512 devices in a mesh: dp: 32 (over z, x_hi), tensor: 16 (over x_lo, y, core).
Axes of the slice: x: 4 (x_hi: 2, x_lo: 2; x = x_hi * 2 + x_lo), y: 4, z: 16, core: 2. Of those that a mesh axis runs over, the one named last changes fastest.
Arguments:
- tokens: bfloat16 [1024, 16384], P('dp', 'tensor'), may hold values from -6 to 6
- up_weight: bfloat16 [26624, 16384], P('dp', 'tensor'), may hold values from -0.046875 to 0.046875
- angles: float32 [4, 16384], P(None, 'tensor'), may hold values from -0.6 to 0.6
- pair_order: int32 [4, 1024], replicated, may hold values from 0 to 1023, each once within a row
- cotangent: bfloat16 [1024, 26624], P('tensor', 'dp'), may hold values from -0.14648438 to 0.14648438
Outputs:
- projected: bfloat16 [1024, 26624], P('tensor', 'dp')
- angle_grads: float32 [4, 16384], P(None, 'tensor')
The draws below stay inside these ranges and needn't reach their ends.
Inputs may be any that keep to these rules, and one draw needn't show every extreme that they name: Each row of pair_order is a permutation of 0 .. 1023.
All inputs are finite; a program needn't handle non-finite values.
Results may differ from the reference program's by a relative error of at most 0.025.
Values may be sent and summed in bfloat16 or wider, within the bound.
No kernel may reach another device: no remote copies, remote signals or barrier semaphores. Data moves between devices by JAX's collectives and lax.ppermute only.
A program may use at most 128 MiB of HBM per device.

```python
import jax
import jax.numpy as jnp
from jax import lax

D = 16384
F = 26624
SECTIONS = 4
TOKENS = 1024
ROWS = 1024
N_DP = 32
N_TENSOR = 16


def block_scale(rng, extent, cuts, low, top_value):
    def one(dim, parts):
        steps = jax.random.uniform(jax.random.fold_in(jax.random.fold_in(rng, 6), dim), (parts,), jnp.float32, low / len(cuts), top_value / len(cuts))
        return jnp.repeat(jnp.exp(steps), extent[dim] // parts).reshape((-1,) + (1,) * (len(extent) - dim - 1))

    level = one(*cuts[0])
    for cut in cuts[1:]:
        level = level * one(*cut)
    return level


def centred(stream_key, dims, deviation, bound, cuts=(), dtype=jnp.bfloat16):
    drawn = deviation * jax.random.normal(stream_key, dims, jnp.float32)
    if cuts:
        drawn = drawn * block_scale(stream_key, dims, cuts, -0.22, 0.18)
    return jnp.clip(drawn, -bound, bound).astype(dtype)


def setup_inputs(seed: int = 0) -> dict:
    key_list = jax.random.split(jax.random.key(seed), 6)
    tokens = centred(key_list[0], (TOKENS, D), 1.0, 6.0, ((0, 32), (1, 16)))
    up_weight = centred(key_list[1], (F, D), D ** -0.5, 0.046875, ((0, 32), (1, 16)))
    angles = jnp.clip(jax.random.uniform(key_list[2], (SECTIONS, D), jnp.float32, -0.6, 0.6) * block_scale(key_list[2], (SECTIONS, D), ((1, 16),), -0.4, 0.0), -0.6, 0.6)
    pair_order = jax.vmap(lambda own: jax.random.permutation(own, ROWS))(jax.random.split(key_list[3], SECTIONS)).reshape((SECTIONS, ROWS)).astype(jnp.int32)
    cotangent = centred(key_list[4], (TOKENS, F), ((TOKENS * F // D) ** -0.5), 0.14648438, ((0, 16), (1, 32)))
    return dict(tokens=tokens, up_weight=up_weight, angles=angles, pair_order=pair_order, cotangent=cotangent)


def split_pairs(values, section_bit, group_rows):
    stride = 2 ** section_bit
    leading = values.shape[:-1]
    shaped = values.reshape(leading + (values.shape[-1] // (group_rows * stride * 2), 2, stride, group_rows))
    return shaped[..., 0, :, :], shaped[..., 1, :, :]


def join_pairs(lower_rows, upper_rows):
    stacked = jnp.stack([lower_rows, upper_rows], axis=-3)
    return stacked.reshape(stacked.shape[:-4] + (-1,))


def rotate_pair(lower_rows, upper_rows, pair_row, lower_angle, upper_angle):
    partner = jnp.take(upper_rows, pair_row, axis=-1)
    turned = lower_angle + jnp.take(upper_angle, pair_row, axis=-1)
    cosine = jnp.cos(turned)
    sine_part = jnp.sin(turned)
    new_lower = cosine * lower_rows - sine_part * partner
    new_partner = sine_part * lower_rows + cosine * partner
    return new_lower, new_partner, turned


def pair_gradient(new_lower, new_partner, grad_lower, grad_upper, pair_row, turned):
    cosine = jnp.cos(turned)
    sine_part = jnp.sin(turned)
    partner_grad = jnp.take(grad_upper, pair_row, axis=-1)
    angle_grad = jnp.sum(partner_grad * new_lower - grad_lower * new_partner, axis=0)
    before_lower = cosine * grad_lower + sine_part * partner_grad
    before_partner = cosine * partner_grad - sine_part * grad_lower
    return angle_grad, before_lower, before_partner


def section_forward(values, section_angles, pair_row, inverse, section_bit):
    group_rows = pair_row.shape[0]
    lower_rows, upper_rows = split_pairs(values, section_bit, group_rows)
    lower_angle, upper_angle = split_pairs(section_angles, section_bit, group_rows)
    new_lower, new_partner, turned = rotate_pair(lower_rows, upper_rows, pair_row, lower_angle, upper_angle)
    return join_pairs(new_lower, jnp.take(new_partner, inverse, axis=-1)), (new_lower, new_partner, turned)


def section_backward(stored, gradient, pair_row, inverse, section_bit):
    group_rows = pair_row.shape[0]
    new_lower, new_partner, turned = stored
    grad_lower, grad_upper = split_pairs(gradient, section_bit, group_rows)
    angle_grad, before_lower, before_partner = pair_gradient(new_lower, new_partner, grad_lower, grad_upper, pair_row, turned)
    angle_full = join_pairs(angle_grad, jnp.take(angle_grad, inverse, axis=-1))
    grad_full = join_pairs(before_lower, jnp.take(before_partner, inverse, axis=-1))
    return angle_full, grad_full


def reference(tokens, up_weight, angles, pair_order, cotangent):
    group_rows = D // N_TENSOR
    bit_count = N_TENSOR.bit_length() - 1
    section_bits = [(bit_count - 1 - factor) % bit_count for factor in range(SECTIONS)]
    inverses = [jnp.argsort(pair_order[factor]).astype(jnp.int32) for factor in range(SECTIONS)]
    current = tokens.astype(jnp.float32)
    stored = []
    for factor in range(SECTIONS):
        current, pieces = section_forward(current, angles[factor], pair_order[factor], inverses[factor], section_bits[factor])
        stored.append(pieces)
    rotated = current.astype(jnp.bfloat16)

    def add_group(group_index, running):
        first = group_index * group_rows
        left = lax.dynamic_slice_in_dim(rotated, first, group_rows, 1).astype(jnp.float32)
        right = lax.dynamic_slice_in_dim(up_weight, first, group_rows, 1).astype(jnp.float32)
        partial_value = lax.dot_general(left, right, (((1,), (1,)), ((), ())), precision=lax.Precision.HIGHEST, preferred_element_type=jnp.float32)
        rounded = lax.optimization_barrier(partial_value.astype(jnp.bfloat16)).astype(jnp.float32)
        return running + rounded

    summed = lax.fori_loop(jnp.int32(0), jnp.int32(N_TENSOR), add_group, jnp.zeros((TOKENS, F), jnp.float32))
    projected = summed.astype(jnp.bfloat16)
    hidden_rows = F // N_DP

    def add_block(block_index, running):
        first = block_index * hidden_rows
        columns = lax.dynamic_slice_in_dim(cotangent, first, hidden_rows, 1).astype(jnp.float32)
        weights = lax.dynamic_slice_in_dim(up_weight, first, hidden_rows, 0).astype(jnp.float32)
        partial_value = jnp.dot(columns, weights, precision=lax.Precision.HIGHEST, preferred_element_type=jnp.float32)
        rounded = lax.optimization_barrier(partial_value.astype(jnp.bfloat16)).astype(jnp.float32)
        return running + rounded

    gradient = lax.fori_loop(jnp.int32(0), jnp.int32(N_DP), add_block, jnp.zeros((TOKENS, D), jnp.float32))
    factor_sums = [None] * SECTIONS
    for factor in reversed(range(SECTIONS)):
        factor_sums[factor], gradient = section_backward(stored[factor], gradient, pair_order[factor], inverses[factor], section_bits[factor])
    return projected, jnp.stack(factor_sums)
```

```python
import functools

import jax
import jax.numpy as jnp
import numpy as np
from jax import lax
from jax.experimental import pallas as pl
from jax.experimental.pallas import tpu as pltpu
from jax.sharding import PartitionSpec as P

BF16 = jnp.bfloat16
F32 = jnp.float32
Z = "z"
TENSOR = ("xl", "y", "c")
NEAR = ("xl", "y")
PLANE = ("xh", "xl", "y", "c")
STEPS = (64, 32, 16, 8, 4, 2)


def all_to_all(array, axes):
    return lax.all_to_all(array, axes, 0, 0, tiled=True)


def split_two(value):
    high = value.astype(BF16)
    low = (value - high.astype(F32)).astype(BF16)
    return high, low


def permuted(value, matrix, transposed):
    rows = value.shape[0]
    both = jnp.concatenate(split_two(value), axis=0)
    dims = (((1,), (1 if transposed else 0,)), ((), ()))
    out = lax.dot_general(both, matrix, dims, preferred_element_type=F32)
    return out[:rows] + out[rows:]


def spread(matrix, value):
    high, low = split_two(value)
    dims = (((1,), (0,)), ((), ()))
    return lax.dot_general(matrix, high, dims, preferred_element_type=F32) + lax.dot_general(
        matrix, low, dims, preferred_element_type=F32
    )


def swap_groups(value, distance):
    rows = value.shape[0]
    if distance < 8:
        parts = [pltpu.roll(value[i : i + 8], 4, 0) for i in range(0, rows, 8)]
    else:
        parts = []
        for i in range(0, rows, 2 * distance):
            parts += [value[i + distance : i + 2 * distance], value[i : i + distance]]
    return jnp.concatenate(parts, axis=0)


def forward_kernel(bits, each, x_ref, low_ref, up_ref, order_ref, pick_ref, mask_ref,
                   z_ref, kept_ref, cos_ref, sin_ref, now):
    step = pl.program_id(0)

    @pl.when(step == 0)
    def _():
        now[...] = x_ref[...].astype(F32)

    order = order_ref[0]
    turned = low_ref[0] + permuted(up_ref[0], order, False)
    cosine = jnp.cos(turned)
    sine = jnp.sin(turned)
    cos_ref[0] = cosine
    sin_ref[0] = sine
    cos_rows = spread(pick_ref[0, 0], cosine)
    sin_rows = spread(pick_ref[0, 1], sine)
    upper = mask_ref[0][:, :1] > 0
    value = now[...]
    value = jnp.where(upper, permuted(value, order, False), value)
    now[...] = value
    for index, bit in enumerate(bits):

        @pl.when(step == index)
        def _():
            kept_ref[0] = cos_rows * now[...] + sin_rows * swap_groups(now[...], each << bit)

    value = kept_ref[0]
    value = jnp.where(upper, permuted(value, order, True), value)
    now[...] = value

    @pl.when(step == len(bits) - 1)
    def _():
        z_ref[...] = value.astype(BF16)


def backward_kernel(bits, each, g_ref, kept_ref, cos_ref, sin_ref, order_ref, pick_ref, sum_ref,
                    mask_ref, low_ref, up_ref, now, other, pair):
    step = pl.program_id(0)

    @pl.when(step == 0)
    def _():
        now[...] = g_ref[...].astype(F32)

    order = order_ref[0]
    cos_rows = spread(pick_ref[0, 0], cos_ref[0])
    sin_rows = spread(pick_ref[0, 1], sin_ref[0])
    upper = mask_ref[0][:, :1] > 0
    value = now[...]
    value = jnp.where(upper, permuted(value, order, False), value)
    now[...] = value
    for index, bit in enumerate(reversed(bits)):

        @pl.when(step == index)
        def _():
            other[...] = swap_groups(now[...], each << bit)
            pair[...] = swap_groups(kept_ref[0], each << bit)

    value = now[...]
    partner = other[...]
    terms = partner * kept_ref[0] - value * pair[...]
    sums = spread(sum_ref[0], terms)
    low_ref[0] = sums
    before = cos_rows * value - sin_rows * partner
    rows = value.shape[0]
    back = permuted(jnp.concatenate([before, sums], axis=0), order, True)
    up_ref[0] = back[rows:]
    now[...] = jnp.where(upper, back[:rows], before)


def tables(bits, groups, each):
    sections, rows = len(bits), groups * each
    pick = np.zeros((sections, 2, rows, groups // 2), np.float32)
    total = np.zeros((sections, groups // 2, rows), np.float32)
    mask = np.zeros((sections, rows, 128), np.float32)
    for s, bit in enumerate(bits):
        stride = 1 << bit
        for row in range(rows):
            group = row // each
            is_upper = group // stride % 2
            pair = group // (2 * stride) * stride + group % stride
            pick[s, 0, row, pair] = 1
            pick[s, 1, row, pair] = 1 if is_upper else -1
            mask[s, row] = is_upper
            if not is_upper:
                total[s, pair, row] = 1
    return pick, total, mask


def block(shape, index=lambda s: s):
    rest = (0,) * (len(shape) - 1)
    return pl.BlockSpec(shape, lambda s: (index(s),) + rest)


def whole(shape):
    return pl.BlockSpec(shape, lambda s: (0,) * len(shape))


def turn_forward(bits, each, x, low, up, order, pick, mask):
    sections, width = order.shape[0], order.shape[1]
    rows, pairs = x.shape[0], low.shape[1]
    return pl.pallas_call(
        functools.partial(forward_kernel, bits, each),
        grid=(sections,),
        in_specs=[
            whole((rows, width)),
            block((1, pairs, width)),
            block((1, pairs, width)),
            block((1, width, width)),
            block((1, 2, rows, pairs)),
            block((1, rows, 128)),
        ],
        out_specs=[
            whole((rows, width)),
            block((1, rows, width)),
            block((1, pairs, width)),
            block((1, pairs, width)),
        ],
        out_shape=[
            jax.ShapeDtypeStruct((rows, width), BF16),
            jax.ShapeDtypeStruct((sections, rows, width), F32),
            jax.ShapeDtypeStruct((sections, pairs, width), F32),
            jax.ShapeDtypeStruct((sections, pairs, width), F32),
        ],
        scratch_shapes=[pltpu.VMEM((rows, width), F32)],
        compiler_params=pltpu.CompilerParams(vmem_limit_bytes=32 << 20),
        cost_estimate=pl.CostEstimate(
            flops=sections * 10 * rows * width * width, bytes_accessed=12 << 20, transcendentals=0
        ),
        name="turn_forward",
    )(x, low, up, order, pick, mask)


def turn_backward(bits, each, g, kept, cosine, sine, order, pick, total, mask):
    sections, width = order.shape[0], order.shape[1]
    rows, pairs = g.shape[0], cosine.shape[1]
    last = sections - 1

    def flip(s):
        return last - s

    return pl.pallas_call(
        functools.partial(backward_kernel, bits, each),
        grid=(sections,),
        in_specs=[
            whole((rows, width)),
            block((1, rows, width), flip),
            block((1, pairs, width), flip),
            block((1, pairs, width), flip),
            block((1, width, width), flip),
            block((1, 2, rows, pairs), flip),
            block((1, pairs, rows), flip),
            block((1, rows, 128), flip),
        ],
        out_specs=[block((1, pairs, width), flip), block((1, pairs, width), flip)],
        out_shape=[jax.ShapeDtypeStruct((sections, pairs, width), F32)] * 2,
        scratch_shapes=[pltpu.VMEM((rows, width), F32)] * 3,
        compiler_params=pltpu.CompilerParams(vmem_limit_bytes=32 << 20),
        cost_estimate=pl.CostEstimate(
            flops=sections * 10 * rows * width * width, bytes_accessed=12 << 20, transcendentals=0
        ),
        name="turn_backward",
    )(g, kept, cosine, sine, order, pick, total, mask)


def split_pairs(values, bit):
    stride = 1 << bit
    shaped = values.reshape((-1, 2, stride) + values.shape[1:])
    return (
        shaped[:, 0].reshape((-1,) + values.shape[1:]),
        shaped[:, 1].reshape((-1,) + values.shape[1:]),
    )


def join_pairs(low, up, bit):
    stride = 1 << bit
    shape = low.shape[1:]
    both = jnp.stack([low.reshape((-1, stride) + shape), up.reshape((-1, stride) + shape)], axis=1)
    return both.reshape((-1,) + shape)


def scale_up(value):
    top = jnp.max(jnp.abs(value))
    scale = jnp.float32(1)
    exponent = jnp.float32(0)
    for step in STEPS:
        fits = top * scale * jnp.float32(2.0**step) < 2.0**15
        scale = jnp.where(fits, scale * jnp.float32(2.0**step), scale)
        exponent = jnp.where(fits, exponent + step, exponent)
    return scale, exponent


def scale_down(exponent):
    scale = jnp.ones_like(exponent)
    for step in STEPS:
        takes = exponent >= step
        scale = jnp.where(takes, scale * jnp.float32(2.0**-step), scale)
        exponent = jnp.where(takes, exponent - step, exponent)
    return scale


def per_device(tokens, up_weight, angles, pair_order, cotangent):
    groups = lax.axis_size(TENSOR)
    near = lax.axis_size(NEAR)
    depth = lax.axis_size(Z)
    sides = lax.axis_size("xh")
    width = up_weight.shape[1]
    hidden = up_weight.shape[0]
    sections = pair_order.shape[0]
    bit_count = groups.bit_length() - 1
    bits = [(bit_count - 1 - s) % bit_count for s in range(sections)]
    core = lax.axis_index("c")
    other_core = [(0, 1), (1, 0)]
    rows = cotangent.shape[0]
    own_rows = tokens.shape[0] // groups
    each = sides * own_rows
    pick, total, mask = tables(bits, groups, each)

    mine = cotangent.reshape(sides, groups, own_rows, hidden).transpose(1, 0, 2, 3)
    mine = mine.reshape(1, rows, hidden)
    cot_own = all_to_all(jnp.broadcast_to(mine, (near, rows, hidden)), NEAR)
    cot_other = lax.ppermute(cot_own, "c", other_core)

    def gradient_part(cot):
        return jnp.dot(
            cot.reshape(near * rows, hidden), up_weight, preferred_element_type=F32
        ).astype(BF16).reshape(near, rows, width)

    part_own = gradient_part(cot_own)
    part_other = gradient_part(cot_other)
    is_first = core == 0
    part = jnp.stack(
        [jnp.where(is_first, part_own, part_other), jnp.where(is_first, part_other, part_own)],
        axis=1,
    )
    gradient = lax.psum_scatter(
        part.reshape(depth * rows, width), Z, scatter_dimension=0, tiled=True
    )

    spread_tokens = jnp.broadcast_to(
        tokens.reshape(1, groups, own_rows, width), (sides, groups, own_rows, width)
    ).reshape(sides * groups, own_rows, width)
    got = all_to_all(spread_tokens, PLANE).reshape(sides, groups, own_rows, width)
    x = got.transpose(1, 0, 2, 3).reshape(groups * each, width)
    all_angles = all_to_all(
        jnp.broadcast_to(angles.reshape(1, sections * width), (groups, sections * width)), TENSOR
    ).reshape(groups, sections, width)
    pairs = [split_pairs(all_angles[:, s], bits[s]) for s in range(sections)]
    low = jnp.stack([p[0] for p in pairs])
    up = jnp.stack([p[1] for p in pairs])
    order = (
        lax.broadcasted_iota(jnp.int32, (sections, width, width), 1) == pair_order[:, None, :]
    ).astype(BF16)
    pick = jnp.asarray(pick, BF16)
    total = jnp.asarray(total, BF16)
    mask = jnp.asarray(mask)
    rotated, kept, cosine, sine = turn_forward(bits, each, x, low, up, order, pick, mask)

    back = all_to_all(rotated.reshape(groups, each, width), TENSOR).reshape(rows, width)
    back = back.astype(F32)
    scale, exponent = scale_up(back)
    packed = jnp.concatenate(
        [(back * scale).astype(jnp.float16), jnp.full((rows, 128), exponent, jnp.float16)], axis=1
    )
    token_all = lax.all_gather(packed, Z, axis=0, tiled=True)
    shrink = scale_down(token_all[:, width].astype(F32)).reshape(near, 2, rows, 1)
    token_all = token_all[:, :width].astype(BF16).reshape(near, 2, rows, width)

    def projected_part(which):
        chosen = lax.dynamic_index_in_dim(token_all, which, 1, keepdims=False)
        factor = lax.dynamic_index_in_dim(shrink, which, 1, keepdims=False)
        return factor * lax.dot_general(
            chosen, up_weight, (((2,), (1,)), ((), ())), preferred_element_type=F32
        )

    sent = lax.ppermute(projected_part(1 - core).astype(BF16), "c", other_core)
    both = (projected_part(core).astype(BF16).astype(F32) + sent.astype(F32)).astype(BF16)
    terms = all_to_all(both, NEAR).astype(F32)
    projected = jnp.sum(terms, axis=0).astype(BF16)
    projected = projected.reshape(groups, sides, own_rows, hidden).transpose(1, 0, 2, 3)
    projected = projected.reshape(rows, hidden)

    g = all_to_all(gradient.reshape(groups, each, width), TENSOR).reshape(groups * each, width)
    low_sums, up_sums = turn_backward(
        bits, each, g, kept, cosine, sine, order, pick, total, mask
    )
    sums = jnp.stack(
        [join_pairs(low_sums[s], up_sums[s], bits[s]) for s in range(sections)], axis=1
    ).reshape(1, groups, sections * width)
    sums = jnp.broadcast_to(sums, (sides, groups, sections * width))
    sums = all_to_all(sums.reshape(sides * groups, sections * width), PLANE)
    sums = jnp.sum(sums, axis=0, keepdims=True)
    sums = all_to_all(jnp.broadcast_to(sums, (depth, sections * width)), Z)
    angle_grads = jnp.sum(sums, axis=0).reshape(sections, width)
    return projected, angle_grads


def solution(mesh):
    fine = jax.sharding.Mesh(
        mesh.devices.reshape(16, 2, 2, 4, 2), ("z", "xh", "xl", "y", "c")
    )
    dp, tensor = ("z", "xh"), TENSOR
    placed = (P(dp, tensor), P(dp, tensor), P(None, tensor), P(), P(tensor, dp))
    return jax.shard_map(
        per_device,
        mesh=fine,
        in_specs=placed,
        out_specs=(P(tensor, dp), P(None, tensor)),
        check_vma=False,
    )
```

```python
import functools

import jax
import jax.numpy as jnp
from jax import lax
from jax.experimental import pallas as pl
from jax.experimental.pallas import tpu as pltpu
from jax.sharding import PartitionSpec as P

BF16 = jnp.bfloat16
F16 = jnp.float16
F32 = jnp.float32
Z = "z"
TENSOR = ("xl", "y", "c")
NEAR = ("xl", "y")
PLANE = ("xh", "xl", "y", "c")
STEPS = (64, 32, 16, 8, 4, 2)
LANES = 128
VMEM = 24 << 20


def all_to_all(array, axes):
    return lax.all_to_all(array, axes, 0, 0, tiled=True)


def copies(array, count):
    return jnp.broadcast_to(array[None], (count,) + array.shape).reshape(
        (count * array.shape[0],) + array.shape[1:]
    )


def product(left, right, transposed):
    dims = (((1,), (1 if transposed else 0,)), ((), ()))
    return lax.dot_general(left, right, dims, preferred_element_type=F32)


def permuted(value, matrix, transposed):
    rows = value.shape[0]
    high = value.astype(BF16)
    low = (value - high.astype(F32)).astype(BF16)
    out = product(jnp.concatenate([high, low], axis=0), matrix, transposed)
    return out[:rows] + out[rows:]


def one_hot(order_row):
    width = order_row.shape[1]
    rows = lax.broadcasted_iota(jnp.int32, (width, width), 0)
    return jnp.where(rows == order_row, 1.0, 0.0).astype(BF16)


def upper_rows(rows, groups, stride):
    group = lax.broadcasted_iota(jnp.int32, (rows, 1), 0) & (groups - 1)
    return (group & stride) != 0


def swap_rows(value, distance):
    rows = value.shape[0]
    if distance >= 8:
        parts = []
        for i in range(0, rows, 2 * distance):
            parts += [value[i + distance : i + 2 * distance], value[i : i + distance]]
        return jnp.concatenate(parts, axis=0)
    tiles = []
    lower = (lax.broadcasted_iota(jnp.int32, (8, 1), 0) & distance) == 0
    for i in range(0, rows, 8):
        tile = value[i : i + 8]
        ahead = pltpu.roll(tile, 8 - distance, 0)
        if distance == 4:
            tiles.append(ahead)
        else:
            tiles.append(jnp.where(lower, ahead, pltpu.roll(tile, distance, 0)))
    return jnp.concatenate(tiles, axis=0)


def swap_into(target, value, step, strides):
    for index, stride in enumerate(strides):

        @pl.when(step == index)
        def _():
            target[...] = swap_rows(value, stride)


def tiled_rows(value, count):
    return jnp.concatenate([value] * count, axis=0)


def forward_kernel(strides, groups, each, x_ref, order_ref, after_ref,
                   z_ref, kept_ref, trig_ref, now, swapped, dense, angles):
    step = pl.program_id(0)
    width = order_ref.shape[2]
    rows = groups * each
    parts = width // LANES
    stride = lax.shift_right_logical(jnp.int32(strides[0]), step)

    @pl.when(step == 0)
    def _():
        dense[:, : x_ref.shape[1], :] = x_ref[...].astype(F32)
        for part in range(x_ref.shape[1] // parts):
            for lane in range(parts):
                piece = dense[:, part * parts + lane, :]
                lanes = slice(lane * LANES, (lane + 1) * LANES)
                if part < each:
                    now[part * groups : (part + 1) * groups, lanes] = piece
                else:
                    angles[part - each, :, lanes] = piece

    matrix = one_hot(order_ref[0])
    value = jnp.concatenate([now[...], angles[step]], axis=0)
    upper = upper_rows(rows + groups, groups, stride)
    value = jnp.where(upper, permuted(value, matrix, False), value)
    swap_into(swapped, value, step, strides)
    turned = value[rows:] + swapped[rows:]
    cosine = jnp.cos(turned)
    sine = jnp.sin(turned)
    sine = jnp.where(upper[rows:], sine, -sine)
    trig_ref[0, :groups] = cosine
    trig_ref[0, groups:] = sine
    value = tiled_rows(cosine, each) * value[:rows] + tiled_rows(sine, each) * swapped[:rows]
    kept_ref[0] = value.astype(BF16)
    value = jnp.where(upper[:rows], permuted(value, matrix, True), value)
    now[...] = value

    @pl.when(step == len(strides) - 1)
    def _():
        for part in range(each * parts):
            row, lane = part // parts * groups, part % parts * LANES
            dense[:, part, :] = value[row : row + groups, lane : lane + LANES]
        for side in range(z_ref.shape[0]):
            z_ref[side] = dense[:, : each * parts, :].astype(BF16)


def pack_kernel(in_ref, after_ref, out_ref, dense):
    value = in_ref[...].astype(F32)
    top = jnp.max(jnp.abs(value), axis=(0, 1))
    top = jnp.max(jnp.max(top, axis=0, keepdims=True), axis=1, keepdims=True)
    scale = jnp.ones_like(top)
    exponent = jnp.zeros_like(top)
    for size in STEPS:
        fits = top * scale * 2.0**size < 2.0**15
        scale = jnp.where(fits, scale * 2.0**size, scale)
        exponent = jnp.where(fits, exponent + size, exponent)
    dense[...] = value * scale.reshape(1, 1, 1, 1)
    sides, rows, parts, _ = in_ref.shape
    for part in range(sides * parts):
        out_ref[:, part * LANES : (part + 1) * LANES] = dense[
            part // parts, :, part % parts, :
        ].astype(BF16)
    out_ref[:, sides * parts * LANES :] = jnp.broadcast_to(exponent, (rows, LANES)).astype(BF16)


def pack(array, after):
    sides, rows, parts, _ = array.shape
    return pl.pallas_call(
        pack_kernel,
        in_specs=[
            pl.BlockSpec(memory_space=pltpu.VMEM),
            pl.BlockSpec(memory_space=pl.ANY),
        ],
        out_shape=jax.ShapeDtypeStruct((rows, (sides * parts + 1) * LANES), BF16),
        scratch_shapes=[pltpu.VMEM(array.shape, F32)],
        name="pack",
    )(array, after)


def backward_kernel(strides, groups, each, side_ref, g_ref, own_ref, other_ref, trig_ref, order_ref,
                    sum_ref, now, swapped, dense, sums_out):
    step = pl.program_id(0)
    width = own_ref.shape[2]
    rows = groups * each
    parts = width // LANES
    stride = lax.shift_left(jnp.int32(strides[-1]), step)

    @pl.when(step == 0)
    def _():
        dense[...] = g_ref[...].astype(F32)
        for part in range(each * parts):
            row, lane = part // parts * groups, part % parts * LANES
            now[row : row + groups, lane : lane + LANES] = dense[:, part, :]

    matrix = one_hot(order_ref[0])
    upper = upper_rows(rows + groups, groups, stride)
    value = now[...]
    value = jnp.where(upper[:rows], permuted(value, matrix, False), value)
    own, other = own_ref[0].astype(F32), other_ref[0].astype(F32)
    first = side_ref[0] == 0
    kept = jnp.concatenate([jnp.where(first, own, other), jnp.where(first, other, own)], axis=0)
    swap_into(swapped, jnp.concatenate([value, kept], axis=0), step, strides[::-1])
    partner = swapped[:rows]
    terms = partner * kept - value * swapped[rows:]
    sums = terms[:groups]
    for part in range(1, each):
        sums = sums + terms[part * groups : (part + 1) * groups]
    sums = jnp.where(upper[rows:], -sums, sums)
    cosine, sine = trig_ref[0, :groups], trig_ref[0, groups:]
    before = tiled_rows(cosine, each) * value - tiled_rows(sine, each) * partner
    value = jnp.concatenate([before, sums], axis=0)
    value = jnp.where(upper, permuted(value, matrix, True), value)
    now[...] = value[:rows]
    for index in range(len(strides)):

        @pl.when(step == len(strides) - 1 - index)
        def _():
            for part in range(parts):
                sums_out[:, index * parts + part, :] = value[
                    rows:, part * LANES : (part + 1) * LANES
                ]

    @pl.when(step == len(strides) - 1)
    def _():
        for side in range(sum_ref.shape[0]):
            sum_ref[side] = sums_out[...].astype(BF16)


def turn_forward(strides, groups, each, sides, x, order, after):
    sections, _, width = order.shape
    rows = groups * each
    return pl.pallas_call(
        functools.partial(forward_kernel, strides, groups, each),
        grid=(sections,),
        in_specs=[
            pl.BlockSpec(x.shape, lambda s: (0, 0, 0)),
            pl.BlockSpec((1, 1, width), lambda s: (s, 0, 0)),
            pl.BlockSpec(memory_space=pl.ANY),
        ],
        out_specs=[
            pl.BlockSpec((sides, groups, each * width // LANES, LANES), lambda s: (0, 0, 0, 0)),
            pl.BlockSpec((1, rows, width), lambda s: (s, 0, 0)),
            pl.BlockSpec((1, 2 * groups, width), lambda s: (s, 0, 0)),
        ],
        out_shape=[
            jax.ShapeDtypeStruct((sides, groups, each * width // LANES, LANES), BF16),
            jax.ShapeDtypeStruct((sections, rows, width), BF16),
            jax.ShapeDtypeStruct((sections, 2 * groups, width), F32),
        ],
        scratch_shapes=[
            pltpu.VMEM((rows, width), F32),
            pltpu.VMEM((rows + groups, width), F32),
            pltpu.VMEM((groups, max(x.shape[1], each * width // LANES), LANES), F32),
            pltpu.VMEM((sections, groups, width), F32),
        ],
        compiler_params=pltpu.CompilerParams(vmem_limit_bytes=VMEM),
        cost_estimate=pl.CostEstimate(
            flops=sections * 8 * rows * width * width, bytes_accessed=4 << 20, transcendentals=0
        ),
        name="turn_forward",
    )(x, order, after)


def turn_backward(strides, groups, each, sides, side, g, own, other, trig, order):
    sections, _, width = order.shape
    rows = groups * each
    last = sections - 1
    return pl.pallas_call(
        functools.partial(backward_kernel, strides, groups, each),
        grid=(sections,),
        in_specs=[
            pl.BlockSpec(memory_space=pltpu.SMEM),
            pl.BlockSpec(g.shape, lambda s: (0, 0, 0)),
            pl.BlockSpec((1, rows // sides, width), lambda s: (last - s, 0, 0)),
            pl.BlockSpec((1, rows // sides, width), lambda s: (last - s, 0, 0)),
            pl.BlockSpec((1, 2 * groups, width), lambda s: (last - s, 0, 0)),
            pl.BlockSpec((1, 1, width), lambda s: (last - s, 0, 0)),
        ],
        out_specs=pl.BlockSpec(
            (sides, groups, sections * width // LANES, LANES), lambda s: (0, 0, 0, 0)
        ),
        out_shape=jax.ShapeDtypeStruct(
            (sides, groups, sections * width // LANES, LANES), BF16
        ),
        scratch_shapes=[
            pltpu.VMEM((rows, width), F32),
            pltpu.VMEM((2 * rows, width), F32),
            pltpu.VMEM(g.shape, F32),
            pltpu.VMEM((groups, sections * width // LANES, LANES), F32),
        ],
        compiler_params=pltpu.CompilerParams(vmem_limit_bytes=VMEM),
        cost_estimate=pl.CostEstimate(
            flops=sections * 8 * rows * width * width, bytes_accessed=4 << 20, transcendentals=0
        ),
        name="turn_backward",
    )(side, g, own, other, trig, order)


def gradient_kernel(core_ref, cot_ref, weight_ref, *refs):
    out_ref, dense = refs[-2:]
    near, rows, _ = cot_ref.shape
    hidden, width = weight_ref.shape
    few = out_ref.shape[2]
    parts = width // LANES
    for part in range(rows // few):
        out = product(
            cot_ref[:, part * few : (part + 1) * few, -hidden:].reshape(near * few, hidden),
            weight_ref[...],
            False,
        )
        for lane in range(parts):
            dense[:, part * parts + lane, :] = out[:, lane * LANES : (lane + 1) * LANES]
    out_ref[...] = dense[...].astype(BF16).reshape(out_ref.shape)


def gradient_half(core, cot, weight, each, before=None, after=None):
    near, rows, lanes = cot.shape
    hidden, width = weight.shape
    few = rows // each
    high = each * width // LANES
    in_specs = [
        pl.BlockSpec((near, rows // 2, lanes), lambda e, c: (0, e, 0)),
        pl.BlockSpec((hidden, width), lambda e, c: (0, 0)),
    ]
    operands = [core, cot, weight]
    aliases = {}
    if before is not None:
        in_specs.append(pl.BlockSpec(memory_space=pl.ANY))
        operands.append(before)
        aliases = {3: 0}
    if after is not None:
        in_specs.append(pl.BlockSpec(memory_space=pl.ANY))
        operands.append(after)
    return pl.pallas_call(
        gradient_kernel,
        grid_spec=pltpu.PrefetchScalarGridSpec(
            num_scalar_prefetch=1,
            grid=(2,),
            in_specs=in_specs,
            out_specs=pl.BlockSpec(
                (near, 1, few, high // 2, LANES), lambda e, c: (0, c[0], 0, e, 0)
            ),
            scratch_shapes=[pltpu.VMEM((near * few, high // 2, LANES), F32)],
        ),
        out_shape=jax.ShapeDtypeStruct((near, 2, few, high, LANES), BF16),
        input_output_aliases=aliases,
        compiler_params=pltpu.CompilerParams(vmem_limit_bytes=VMEM),
        cost_estimate=pl.CostEstimate(
            flops=2 * near * rows * hidden * width, bytes_accessed=4 << 20, transcendentals=0
        ),
        name="gradient_half",
    )(*operands)


def projected_kernel(core_ref, token_ref, exponent_ref, weight_ref, *refs):
    out_ref = refs[-1]
    near, _, few, width = token_ref.shape
    tokens = token_ref[...].reshape(near * few, width)
    out = product(tokens, weight_ref[...], True)
    exponent = exponent_ref[...].reshape(near * few, LANES)[:, :1].astype(F32)
    scale = jnp.ones_like(exponent)
    for size in STEPS:
        takes = exponent >= size
        scale = jnp.where(takes, scale * 2.0**-size, scale)
        exponent = jnp.where(takes, exponent - size, exponent)
    out = (out * scale).astype(BF16)
    if len(refs) > 1:
        out = (out.astype(F32) + refs[0][...].reshape(out.shape).astype(F32)).astype(BF16)
    out_ref[...] = out.reshape(out_ref.shape)


def projected_half(core, token_all, weight, each, arrived=None, after=None):
    near, _, few, _ = token_all.shape
    hidden, width = weight.shape
    in_specs = [
        pl.BlockSpec((near, 1, few, width), lambda e, c: (0, c[0], 0, e)),
        pl.BlockSpec((near, 1, few, LANES), lambda e, c: (0, c[0], 0, each * width // LANES)),
        pl.BlockSpec((hidden, width), lambda e, c: (0, 0)),
    ]
    operands = [core, token_all, token_all, weight]
    if arrived is not None:
        in_specs.append(pl.BlockSpec((near, few, hidden), lambda e, c: (0, e, 0)))
        operands.append(arrived)
    if after is not None:
        in_specs.append(pl.BlockSpec(memory_space=pl.ANY))
        operands.append(after)
    return pl.pallas_call(
        projected_kernel,
        grid_spec=pltpu.PrefetchScalarGridSpec(
            num_scalar_prefetch=1,
            grid=(each,),
            in_specs=in_specs,
            out_specs=pl.BlockSpec((near, few, hidden), lambda e, c: (0, e, 0)),
        ),
        out_shape=jax.ShapeDtypeStruct((near, each * few, hidden), BF16),
        compiler_params=pltpu.CompilerParams(vmem_limit_bytes=VMEM),
        cost_estimate=pl.CostEstimate(
            flops=near * few * each * hidden * width // 4, bytes_accessed=1 << 20,
            transcendentals=0,
        ),
        name="projected_half",
    )(*operands)


def sum_kernel(in_ref, out_ref):
    total = jnp.sum(in_ref[...].astype(F32), axis=0).astype(out_ref.dtype)
    for index in range(out_ref.shape[0]):
        out_ref[index] = total


def sum_copies(array, count):
    return pl.pallas_call(
        sum_kernel,
        out_shape=jax.ShapeDtypeStruct((count,) + array.shape[1:], array.dtype),
        name="sum_copies",
    )(array)


def per_device(tokens, up_weight, angles, pair_order, cotangent):
    groups = lax.axis_size(TENSOR)
    near = lax.axis_size(NEAR)
    depth = lax.axis_size(Z)
    sides = lax.axis_size("xh")
    hidden, width = up_weight.shape
    sections = pair_order.shape[0]
    strides = [groups >> (s + 1) for s in range(sections)]
    own_rows = tokens.shape[0] // groups
    each = sides * own_rows
    core = lax.axis_index("c").astype(jnp.int32).reshape(1)
    other_core = [(0, 1), (1, 0)]
    order = pair_order.reshape(sections, 1, width)

    parts = width // LANES
    few = tokens.reshape(own_rows, near, 2, width).transpose(1, 2, 0, 3)
    few = few.reshape(near, 2 * own_rows, width)
    few = jnp.concatenate([few, copies(angles.astype(BF16)[None], near)], axis=1)
    few = few.reshape(near, (2 * own_rows + sections) * parts, LANES)
    mine = jnp.concatenate([few, copies(cotangent[None], near)], axis=2)
    cot_own = all_to_all(mine, NEAR)
    cot_other = lax.ppermute(cot_own, "c", other_core)

    def of_this_core(array):
        start = core[0] * own_rows * parts
        return jnp.concatenate(
            [
                lax.dynamic_slice_in_dim(array[:, :, :LANES], start, own_rows * parts, 1),
                array[:, 2 * own_rows * parts :, :LANES],
            ],
            axis=1,
        )

    def in_order(which, own, other, axis):
        return jnp.stack(
            [jnp.where(which == 0, own, other), jnp.where(which == 0, other, own)], axis=axis
        )

    x = in_order(core[0], of_this_core(cot_own), of_this_core(cot_other), 1)
    x = x.reshape(groups, (own_rows + sections) * parts, LANES)

    part = gradient_half(core, cot_own, up_weight, each)
    part = gradient_half(1 - core, cot_other, up_weight, each, part)
    gradient = lax.psum_scatter(
        part.reshape(depth * groups, each * width // LANES, LANES),
        Z,
        scatter_dimension=0,
        tiled=True,
    )

    rotated, kept, trig = turn_forward(
        strides, groups, own_rows, sides, x, order, part
    )
    other_kept = lax.ppermute(kept, "xh", other_core)
    back = all_to_all(rotated.reshape((sides * groups,) + rotated.shape[2:]), PLANE)
    back = pack(back.reshape(rotated.shape), other_kept).astype(F16)
    token_all = lax.all_gather(back, Z, axis=0, tiled=True).astype(BF16)
    token_all = token_all.reshape(near, 2, groups, each * width + LANES)

    g = all_to_all(gradient, TENSOR)

    side = lax.axis_index("xh").astype(jnp.int32).reshape(1)
    sums = turn_backward(
        strides, groups, each, sides, side, g, kept, other_kept, trig, order
    )

    sent = projected_half(1 - core, token_all, up_weight, each)
    arrived = lax.ppermute(sent, "c", other_core)
    both = projected_half(core, token_all, up_weight, each, arrived)
    projected = lax.psum_scatter(
        both.reshape(near * each * groups, hidden), NEAR, scatter_dimension=0, tiled=True
    )

    sums = all_to_all(sums.reshape((sides * groups,) + sums.shape[2:]), PLANE)
    sums = all_to_all(sum_copies(sums, depth), Z)
    angle_grads = jnp.sum(sums.astype(F32), axis=0).reshape(sections, width)
    return projected, angle_grads


def solution(mesh):
    fine = jax.sharding.Mesh(
        mesh.devices.reshape(16, 2, 2, 4, 2), ("z", "xh", "xl", "y", "c")
    )
    dp, tensor = ("z", "xh"), TENSOR
    placed = (P(dp, tensor), P(dp, tensor), P(None, tensor), P(), P(tensor, dp))
    return jax.shard_map(
        per_device,
        mesh=fine,
        in_specs=placed,
        out_specs=(P(tensor, dp), P(None, tensor)),
        check_vma=False,
    )
```

```python
import functools

import jax
import jax.numpy as jnp
from jax import lax
from jax.experimental import pallas as pl
from jax.experimental.pallas import tpu as pltpu
from jax.sharding import PartitionSpec as P

BF16 = jnp.bfloat16
F16 = jnp.float16
F32 = jnp.float32
Z = "z"
TENSOR = ("xl", "y", "c")
NEAR = ("xl", "y")
PLANE = ("xh", "xl", "y", "c")
STEPS = (64, 32, 16, 8, 4, 2)
LANES = 128
VMEM = 24 << 20


def all_to_all(array, axes):
    return lax.all_to_all(array, axes, 0, 0, tiled=True)


def product(left, right, transposed):
    dims = (((1,), (1 if transposed else 0,)), ((), ()))
    return lax.dot_general(left, right, dims, preferred_element_type=F32)


def permuted(value, order):
    rows, width = value.shape
    tiles = width // LANES
    out = []
    for to in range(tiles):
        index = order[:, to * LANES : (to + 1) * LANES]
        lane = jnp.broadcast_to(index & (LANES - 1), (rows, LANES))
        tile = jnp.broadcast_to(index // LANES, (rows, LANES))
        chosen = None
        for source in range(tiles):
            piece = jnp.take_along_axis(
                value[:, source * LANES : (source + 1) * LANES],
                lane,
                axis=1,
                mode="promise_in_bounds",
            )
            chosen = piece if chosen is None else jnp.where(tile == source, piece, chosen)
        out.append(chosen)
    return jnp.concatenate(out, axis=1)


def inverse_kernel(column_ref, row_ref, out_ref):
    width, sections = column_ref.shape
    row = lax.broadcasted_iota(jnp.int32, (width, width), 0)
    lane = lax.broadcasted_iota(jnp.int32, (width, width), 1)
    for s in range(sections):
        hits = jnp.where(column_ref[:, s : s + 1] == lane, row, 0)
        out_ref[s, 0:1] = row_ref[s : s + 1]
        out_ref[s, 1:2] = jnp.sum(hits, axis=0, keepdims=True)


def with_inverses(order):
    sections, width = order.shape
    return pl.pallas_call(
        inverse_kernel,
        out_shape=jax.ShapeDtypeStruct((sections, 2, width), jnp.int32),
        compiler_params=pltpu.CompilerParams(vmem_limit_bytes=VMEM),
        name="with_inverses",
    )(order.T, order)


def prepare_kernel(token_ref, angle_ref, cot_ref, out_ref, tokens, dense):
    near = out_ref.shape[0]
    groups, width = 2 * near, token_ref.shape[1]
    own_rows = token_ref.shape[0] // groups
    parts = width // LANES
    for part in range(parts):
        lanes = slice(part * LANES, (part + 1) * LANES)
        tokens[part] = token_ref[:, lanes].astype(F32)
        for core in range(2):
            for row in range(own_rows):
                dense[:, (core * own_rows + row) * parts + part, :] = tokens[
                    part, pl.ds(row * groups + core, near, stride=2), :
                ]
        for s in range(angle_ref.shape[0]):
            dense[:, (2 * own_rows + s) * parts + part, :] = jnp.broadcast_to(
                angle_ref[s : s + 1, lanes], (near, LANES)
            )
    out_ref[:, :, :LANES] = dense[...].astype(BF16)
    for index in range(near):
        out_ref[index, :, LANES:] = cot_ref[...]


def prepare(tokens, angles, cotangent, near):
    rows, hidden = cotangent.shape
    return pl.pallas_call(
        prepare_kernel,
        out_shape=jax.ShapeDtypeStruct((near, rows, LANES + hidden), BF16),
        scratch_shapes=[pltpu.VMEM((tokens.shape[1] // LANES, tokens.shape[0], LANES), F32), pltpu.VMEM((near, rows, LANES), F32)],
        compiler_params=pltpu.CompilerParams(vmem_limit_bytes=60 << 20),
        name="prepare",
    )(tokens, angles, cotangent)


def upper_rows(rows, groups, stride):
    group = lax.broadcasted_iota(jnp.int32, (rows, 1), 0) & (groups - 1)
    return (group & stride) != 0


def swap_rows(value, distance):
    rows = value.shape[0]
    if distance >= 8:
        parts = []
        for i in range(0, rows, 2 * distance):
            parts += [value[i + distance : i + 2 * distance], value[i : i + distance]]
        return jnp.concatenate(parts, axis=0)
    tiles = []
    lower = (lax.broadcasted_iota(jnp.int32, (8, 1), 0) & distance) == 0
    for i in range(0, rows, 8):
        tile = value[i : i + 8]
        ahead = pltpu.roll(tile, 8 - distance, 0)
        if distance == 4:
            tiles.append(ahead)
        else:
            tiles.append(jnp.where(lower, ahead, pltpu.roll(tile, distance, 0)))
    return jnp.concatenate(tiles, axis=0)


def swap_into(target, value, step, strides):
    for index, stride in enumerate(strides):

        @pl.when(step == index)
        def _():
            target[...] = swap_rows(value, stride)


def tiled_rows(value, count):
    return jnp.concatenate([value] * count, axis=0)


def forward_kernel(strides, groups, each, core_ref, own_ref, other_ref, order_ref, after_ref,
                   z_ref, kept_ref, trig_ref, now, swapped, dense, angles):
    step = pl.program_id(0)
    width = order_ref.shape[2]
    rows = groups * each
    parts = width // LANES
    stride = lax.shift_right_logical(jnp.int32(strides[0]), step)

    @pl.when(step == 0)
    def _():
        core = core_ref[0]
        tall = each * parts
        for which, ref in ((core, own_ref), (1 - core, other_ref)):
            tokens = ref[:, pl.ds(pl.multiple_of(core * tall, tall), tall), :].astype(F32)
            rest = ref[:, 2 * tall :, :].astype(F32)
            for near in range(groups // 2):
                dense[pl.ds(2 * near + which, 1), :tall] = tokens[near : near + 1]
                dense[pl.ds(2 * near + which, 1), tall:] = rest[near : near + 1]
        for part in range(each + len(strides)):
            for lane in range(parts):
                piece = dense[:, part * parts + lane, :]
                lanes = slice(lane * LANES, (lane + 1) * LANES)
                if part < each:
                    now[part * groups : (part + 1) * groups, lanes] = piece
                else:
                    angles[part - each, :, lanes] = piece

    order, inverse = order_ref[0, 0:1], order_ref[0, 1:2]
    value = jnp.concatenate([now[...], angles[step]], axis=0)
    upper = upper_rows(rows + groups, groups, stride)
    value = jnp.where(upper, permuted(value, order), value)
    swap_into(swapped, value, step, strides)
    turned = value[rows:] + swapped[rows:]
    cosine = jnp.cos(turned)
    sine = jnp.sin(turned)
    sine = jnp.where(upper[rows:], sine, -sine)
    trig_ref[0, :groups] = cosine
    trig_ref[0, groups:] = sine
    value = tiled_rows(cosine, each) * value[:rows] + tiled_rows(sine, each) * swapped[:rows]
    kept_ref[0] = value.astype(BF16)
    value = jnp.where(upper[:rows], permuted(value, inverse), value)
    now[...] = value

    @pl.when(step == len(strides) - 1)
    def _():
        for part in range(each * parts):
            row, lane = part // parts * groups, part % parts * LANES
            dense[:, part, :] = value[row : row + groups, lane : lane + LANES]
        for side in range(z_ref.shape[0]):
            z_ref[side] = dense[:, : each * parts, :].astype(BF16)


def pack_kernel(in_ref, out_ref, dense):
    value = in_ref[...].astype(F32)
    top = jnp.max(jnp.abs(value), axis=(0, 1))
    top = jnp.max(jnp.max(top, axis=0, keepdims=True), axis=1, keepdims=True)
    scale = jnp.ones_like(top)
    exponent = jnp.zeros_like(top)
    for size in STEPS:
        fits = top * scale * 2.0**size < 2.0**15
        scale = jnp.where(fits, scale * 2.0**size, scale)
        exponent = jnp.where(fits, exponent + size, exponent)
    dense[...] = value * scale.reshape(1, 1, 1, 1)
    sides, rows, parts, _ = in_ref.shape
    for part in range(sides * parts):
        out_ref[:, part * LANES : (part + 1) * LANES] = dense[
            part // parts, :, part % parts, :
        ].astype(BF16)
    out_ref[:, sides * parts * LANES :] = jnp.broadcast_to(exponent, (rows, LANES)).astype(BF16)


def pack(array):
    sides, rows, parts, _ = array.shape
    return pl.pallas_call(
        pack_kernel,
        out_shape=jax.ShapeDtypeStruct((rows, (sides * parts + 1) * LANES), BF16),
        scratch_shapes=[pltpu.VMEM(array.shape, F32)],
        name="pack",
    )(array)


def backward_kernel(strides, groups, each, g_ref, kept_ref, trig_ref, order_ref,
                    sum_ref, now, swapped, dense, sums_out):
    step = pl.program_id(0)
    width = kept_ref.shape[2]
    rows = groups * each
    parts = width // LANES
    stride = lax.shift_left(jnp.int32(strides[-1]), step)

    @pl.when(step == 0)
    def _():
        dense[...] = jnp.sum(g_ref[...].astype(F32), axis=0)
        for part in range(each * parts):
            row, lane = part // parts * groups, part % parts * LANES
            now[row : row + groups, lane : lane + LANES] = dense[:, part, :]

    order, inverse = order_ref[0, 0:1], order_ref[0, 1:2]
    upper = upper_rows(rows + groups, groups, stride)
    value = now[...]
    value = jnp.where(upper[:rows], permuted(value, order), value)
    kept = kept_ref[0].astype(F32)
    swap_into(swapped, jnp.concatenate([value, kept], axis=0), step, strides[::-1])
    partner = swapped[:rows]
    terms = partner * kept - value * swapped[rows:]
    sums = terms[:groups]
    for part in range(1, each):
        sums = sums + terms[part * groups : (part + 1) * groups]
    sums = jnp.where(upper[rows:], -sums, sums)
    cosine, sine = trig_ref[0, :groups], trig_ref[0, groups:]
    before = tiled_rows(cosine, each) * value - tiled_rows(sine, each) * partner
    value = jnp.concatenate([before, sums], axis=0)
    value = jnp.where(upper, permuted(value, inverse), value)
    now[...] = value[:rows]
    for index in range(len(strides)):

        @pl.when(step == len(strides) - 1 - index)
        def _():
            for part in range(parts):
                sums_out[:, index * parts + part, :] = value[
                    rows:, part * LANES : (part + 1) * LANES
                ]

    @pl.when(step == len(strides) - 1)
    def _():
        for side in range(sum_ref.shape[0]):
            sum_ref[side] = sums_out[...].astype(BF16)


def turn_forward(strides, groups, each, sides, core, own, other, order, after):
    sections, _, width = order.shape
    rows = groups * each
    near, high, _ = own.shape
    return pl.pallas_call(
        functools.partial(forward_kernel, strides, groups, each),
        grid=(sections,),
        in_specs=[
            pl.BlockSpec(memory_space=pltpu.SMEM),
            pl.BlockSpec((near, high, LANES), lambda s: (0, 0, 0)),
            pl.BlockSpec((near, high, LANES), lambda s: (0, 0, 0)),
            pl.BlockSpec((1, 2, width), lambda s: (s, 0, 0)),
            pl.BlockSpec(memory_space=pl.ANY),
        ],
        out_specs=[
            pl.BlockSpec((sides, groups, each * width // LANES, LANES), lambda s: (0, 0, 0, 0)),
            pl.BlockSpec((1, rows, width), lambda s: (s, 0, 0)),
            pl.BlockSpec((1, 2 * groups, width), lambda s: (s, 0, 0)),
        ],
        out_shape=[
            jax.ShapeDtypeStruct((sides, groups, each * width // LANES, LANES), BF16),
            jax.ShapeDtypeStruct((sections, rows, width), BF16),
            jax.ShapeDtypeStruct((sections, 2 * groups, width), F32),
        ],
        scratch_shapes=[
            pltpu.VMEM((rows, width), F32),
            pltpu.VMEM((rows + groups, width), F32),
            pltpu.VMEM((groups, (each + sections) * width // LANES, LANES), F32),
            pltpu.VMEM((sections, groups, width), F32),
        ],
        compiler_params=pltpu.CompilerParams(vmem_limit_bytes=VMEM),
        cost_estimate=pl.CostEstimate(
            flops=sections * 8 * rows * width * width, bytes_accessed=4 << 20, transcendentals=0
        ),
        name="turn_forward",
    )(core, own, other, order, after)


def turn_backward(strides, groups, each, sides, g, kept, trig, order):
    sections, _, width = order.shape
    rows = groups * each
    last = sections - 1
    return pl.pallas_call(
        functools.partial(backward_kernel, strides, groups, each),
        grid=(sections,),
        in_specs=[
            pl.BlockSpec(g.shape, lambda s: (0, 0, 0, 0)),
            pl.BlockSpec((1, rows, width), lambda s: (last - s, 0, 0)),
            pl.BlockSpec((1, 2 * groups, width), lambda s: (last - s, 0, 0)),
            pl.BlockSpec((1, 2, width), lambda s: (last - s, 0, 0)),
        ],
        out_specs=pl.BlockSpec(
            (sides, groups, sections * width // LANES, LANES), lambda s: (0, 0, 0, 0)
        ),
        out_shape=jax.ShapeDtypeStruct(
            (sides, groups, sections * width // LANES, LANES), BF16
        ),
        scratch_shapes=[
            pltpu.VMEM((rows, width), F32),
            pltpu.VMEM((2 * rows, width), F32),
            pltpu.VMEM(g.shape[1:], F32),
            pltpu.VMEM((groups, sections * width // LANES, LANES), F32),
        ],
        compiler_params=pltpu.CompilerParams(vmem_limit_bytes=VMEM),
        cost_estimate=pl.CostEstimate(
            flops=sections * 8 * rows * width * width, bytes_accessed=4 << 20, transcendentals=0
        ),
        name="turn_backward",
    )(g, kept, trig, order)


def gradient_kernel(core_ref, own_ref, other_ref, weight_ref, after_ref, out_ref):
    near, rows, _ = own_ref.shape
    hidden, width = weight_ref.shape
    core = core_ref[0]
    for which, ref in ((core, own_ref), (1 - core, other_ref)):
        out = product(
            ref[:, :, -hidden:].reshape(near * rows, hidden), weight_ref[...], False
        )
        out_ref[:, pl.ds(which, 1)] = out.astype(BF16).reshape(near, 1, rows, width)


def gradient(core, own, other, weight, after):
    near, rows, lanes = own.shape
    hidden, width = weight.shape
    steps = 2
    return pl.pallas_call(
        gradient_kernel,
        grid=(steps,),
        in_specs=[
            pl.BlockSpec(memory_space=pltpu.SMEM),
            pl.BlockSpec((near, rows // steps, lanes), lambda e: (0, e, 0)),
            pl.BlockSpec((near, rows // steps, lanes), lambda e: (0, e, 0)),
            pl.BlockSpec((hidden, width), lambda e: (0, 0)),
            pl.BlockSpec(memory_space=pl.ANY),
        ],
        out_specs=pl.BlockSpec((near, 2, rows // steps, width), lambda e: (0, 0, e, 0)),
        out_shape=jax.ShapeDtypeStruct((near, 2, rows, width), BF16),
        compiler_params=pltpu.CompilerParams(vmem_limit_bytes=VMEM),
        cost_estimate=pl.CostEstimate(
            flops=4 * near * rows * hidden * width, bytes_accessed=6 << 20, transcendentals=0
        ),
        name="gradient",
    )(core, own, other, weight, after)


def spread_kernel(in_ref, out_ref, dense):
    groups = out_ref.shape[1]
    parts = in_ref.shape[1] // LANES
    own_rows = out_ref.shape[2] // parts
    for side in range(out_ref.shape[0]):
        for row in range(own_rows):
            first = (side * own_rows + row) * groups
            for part in range(parts):
                dense[side, :, row * parts + part, :] = in_ref[
                    first : first + groups, part * LANES : (part + 1) * LANES
                ].astype(F32)
    out_ref[...] = dense[...].astype(BF16)


def spread(array, sides, groups):
    rows, width = array.shape
    shape = (sides, groups, rows // (sides * groups) * width // LANES, LANES)
    return pl.pallas_call(
        spread_kernel,
        out_shape=jax.ShapeDtypeStruct(shape, BF16),
        scratch_shapes=[pltpu.VMEM(shape, F32)],
        name="spread",
    )(array)


def projected_kernel(core_ref, token_ref, exponent_ref, weight_ref, *refs):
    out_ref = refs[-1]
    near, _, few, lanes = token_ref.shape
    width = weight_ref.shape[1]
    parts = lanes // width
    tokens = jnp.concatenate(
        [
            token_ref[:, :, :, part * width : (part + 1) * width].reshape(near * few, width)
            for part in range(parts)
        ],
        axis=0,
    )
    out = product(tokens, weight_ref[...], True)
    exponent = exponent_ref[...].reshape(near * few, LANES)[:, :1].astype(F32)
    scale = jnp.ones_like(exponent)
    for size in STEPS:
        takes = exponent >= size
        scale = jnp.where(takes, scale * 2.0**-size, scale)
        exponent = jnp.where(takes, exponent - size, exponent)
    for part in range(parts):
        piece = (out[part * near * few : (part + 1) * near * few] * scale).astype(BF16)
        piece = piece.reshape(near, few, piece.shape[1])
        rows = slice(part * few, (part + 1) * few)
        if len(refs) > 1:
            piece = (piece.astype(F32) + refs[0][:, rows].astype(F32)).astype(BF16)
        out_ref[:, rows] = piece


def projected_half(core, token_all, weight, each, arrived=None, after=None):
    near, _, few, _ = token_all.shape
    hidden, width = weight.shape
    steps = 2
    at_once = each // steps
    in_specs = [
        pl.BlockSpec((near, 1, few, at_once * width), lambda e, c: (0, c[0], 0, e)),
        pl.BlockSpec((near, 1, few, LANES), lambda e, c: (0, c[0], 0, each * width // LANES)),
        pl.BlockSpec((hidden, width), lambda e, c: (0, 0)),
    ]
    operands = [core, token_all, token_all, weight]
    if arrived is not None:
        in_specs.append(pl.BlockSpec((near, at_once * few, hidden), lambda e, c: (0, e, 0)))
        operands.append(arrived)
        in_specs.append(pl.BlockSpec(memory_space=pl.ANY))
        operands.append(after)
    return pl.pallas_call(
        projected_kernel,
        grid_spec=pltpu.PrefetchScalarGridSpec(
            num_scalar_prefetch=1,
            grid=(steps,),
            in_specs=in_specs,
            out_specs=pl.BlockSpec((near, at_once * few, hidden), lambda e, c: (0, e, 0)),
        ),
        out_shape=jax.ShapeDtypeStruct((near, each * few, hidden), BF16),
        compiler_params=pltpu.CompilerParams(vmem_limit_bytes=VMEM),
        cost_estimate=pl.CostEstimate(
            flops=near * few * each * hidden * width // 4, bytes_accessed=1 << 20,
            transcendentals=0,
        ),
        name="projected_half",
    )(*operands)


def sum_kernel(in_ref, out_ref):
    total = jnp.sum(in_ref[...].astype(F32), axis=0).astype(out_ref.dtype)
    for index in range(out_ref.shape[0]):
        out_ref[index] = total


def sum_copies(array, count):
    return pl.pallas_call(
        sum_kernel,
        out_shape=jax.ShapeDtypeStruct((count,) + array.shape[1:], array.dtype),
        name="sum_copies",
    )(array)


def per_device(tokens, up_weight, angles, pair_order, cotangent):
    groups = lax.axis_size(TENSOR)
    near = lax.axis_size(NEAR)
    depth = lax.axis_size(Z)
    sides = lax.axis_size("xh")
    hidden, width = up_weight.shape
    sections = pair_order.shape[0]
    strides = [groups >> (s + 1) for s in range(sections)]
    own_rows = tokens.shape[0] // groups
    each = sides * own_rows
    core = lax.axis_index("c").astype(jnp.int32).reshape(1)
    other_core = [(0, 1), (1, 0)]
    order = with_inverses(pair_order)

    mine = prepare(tokens, angles, cotangent, near)
    cot_own = all_to_all(mine, NEAR)
    cot_other = lax.ppermute(cot_own, "c", other_core)

    part = gradient(core, cot_own, cot_other, up_weight, order)
    summed = lax.psum_scatter(
        part.reshape(depth * part.shape[2], width), Z, scatter_dimension=0, tiled=True
    )

    rotated, kept, trig = turn_forward(
        strides, groups, own_rows, sides, core, cot_own, cot_other, order, part
    )
    back = all_to_all(rotated.reshape((sides * groups,) + rotated.shape[2:]), PLANE)
    back = pack(back.reshape(rotated.shape)).astype(F16)
    token_all = lax.all_gather(back, Z, axis=0, tiled=True).astype(BF16)
    token_all = token_all.reshape(near, 2, groups, each * width + LANES)

    g = spread(summed, sides, groups)

    sent = projected_half(1 - core, token_all, up_weight, each)
    arrived = lax.ppermute(sent, "c", other_core)
    both = projected_half(core, token_all, up_weight, each, arrived, g)
    projected = lax.psum_scatter(
        both.reshape(near * each * groups, hidden), NEAR, scatter_dimension=0, tiled=True
    )

    g = all_to_all(g.reshape((sides * groups,) + g.shape[2:]), PLANE).reshape(rotated.shape)
    sums = turn_backward(strides, groups, own_rows, sides, g, kept, trig, order)

    sums = all_to_all(sums.reshape((sides * groups,) + sums.shape[2:]), PLANE)
    sums = all_to_all(sum_copies(sums, depth), Z)
    angle_grads = jnp.sum(sums.astype(F32), axis=0).reshape(sections, width)
    return projected, angle_grads


def solution(mesh):
    fine = jax.sharding.Mesh(
        mesh.devices.reshape(16, 2, 2, 4, 2), ("z", "xh", "xl", "y", "c")
    )
    dp, tensor = ("z", "xh"), TENSOR
    placed = (P(dp, tensor), P(dp, tensor), P(None, tensor), P(), P(tensor, dp))
    return jax.shard_map(
        per_device,
        mesh=fine,
        in_specs=placed,
        out_specs=(P(tensor, dp), P(None, tensor)),
        check_vma=False,
    )
```

```python
import functools

import jax
import jax.numpy as jnp
from jax import lax
from jax.experimental import pallas as pl
from jax.experimental.pallas import tpu as pltpu
from jax.sharding import PartitionSpec as P

BF16 = jnp.bfloat16
F16 = jnp.float16
F32 = jnp.float32
Z = "z"
TENSOR = ("xl", "y", "c")
NEAR = ("xl", "y")
PLANE = ("xh", "xl", "y", "c")
STEPS = (64, 32, 16, 8, 4, 2)
LANES = 128
VMEM = 24 << 20


def all_to_all(array, axes):
    return lax.all_to_all(array, axes, 0, 0, tiled=True)


def product(left, right, transposed):
    dims = (((1,), (1 if transposed else 0,)), ((), ()))
    return lax.dot_general(left, right, dims, preferred_element_type=F32)


def permuted(value, order):
    rows, width = value.shape
    tiles = width // LANES
    out = []
    for to in range(tiles):
        index = order[:, to * LANES : (to + 1) * LANES]
        lane = jnp.broadcast_to(index & (LANES - 1), (rows, LANES))
        tile = jnp.broadcast_to(index // LANES, (rows, LANES))
        chosen = None
        for source in range(tiles):
            piece = jnp.take_along_axis(
                value[:, source * LANES : (source + 1) * LANES],
                lane,
                axis=1,
                mode="promise_in_bounds",
            )
            chosen = piece if chosen is None else jnp.where(tile == source, piece, chosen)
        out.append(chosen)
    return jnp.concatenate(out, axis=1)


def inverse_kernel(column_ref, row_ref, out_ref):
    width, sections = column_ref.shape
    row = lax.broadcasted_iota(jnp.int32, (width, width), 0)
    lane = lax.broadcasted_iota(jnp.int32, (width, width), 1)
    for s in range(sections):
        hits = jnp.where(column_ref[:, s : s + 1] == lane, row, 0)
        out_ref[s, 0:1] = row_ref[s : s + 1]
        out_ref[s, 1:2] = jnp.sum(hits, axis=0, keepdims=True)


def with_inverses(order):
    sections, width = order.shape
    return pl.pallas_call(
        inverse_kernel,
        out_shape=jax.ShapeDtypeStruct((sections, 2, width), jnp.int32),
        compiler_params=pltpu.CompilerParams(vmem_limit_bytes=VMEM),
        name="with_inverses",
    )(order.T, order)


def prepare_kernel(token_ref, angle_ref, cot_ref, out_ref, tokens, dense):
    near = out_ref.shape[0]
    groups, width = 2 * near, token_ref.shape[1]
    own_rows = token_ref.shape[0] // groups
    parts = width // LANES
    for part in range(parts):
        lanes = slice(part * LANES, (part + 1) * LANES)
        tokens[part] = token_ref[:, lanes].astype(F32)
        for core in range(2):
            for row in range(own_rows):
                dense[:, (core * own_rows + row) * parts + part, :] = tokens[
                    part, pl.ds(row * groups + core, near, stride=2), :
                ]
        for s in range(angle_ref.shape[0]):
            dense[:, (2 * own_rows + s) * parts + part, :] = jnp.broadcast_to(
                angle_ref[s : s + 1, lanes], (near, LANES)
            )
    out_ref[:, :, :LANES] = dense[...].astype(BF16)
    for index in range(near):
        out_ref[index, :, LANES:] = cot_ref[...]


def prepare(tokens, angles, cotangent, near):
    rows, hidden = cotangent.shape
    return pl.pallas_call(
        prepare_kernel,
        out_shape=jax.ShapeDtypeStruct((near, rows, LANES + hidden), BF16),
        scratch_shapes=[pltpu.VMEM((tokens.shape[1] // LANES, tokens.shape[0], LANES), F32), pltpu.VMEM((near, rows, LANES), F32)],
        compiler_params=pltpu.CompilerParams(vmem_limit_bytes=60 << 20),
        name="prepare",
    )(tokens, angles, cotangent)


def upper_rows(rows, groups, stride):
    group = lax.broadcasted_iota(jnp.int32, (rows, 1), 0) & (groups - 1)
    return (group & stride) != 0


def swap_rows(value, distance):
    rows = value.shape[0]
    if distance >= 8:
        parts = []
        for i in range(0, rows, 2 * distance):
            parts += [value[i + distance : i + 2 * distance], value[i : i + distance]]
        return jnp.concatenate(parts, axis=0)
    tiles = []
    lower = (lax.broadcasted_iota(jnp.int32, (8, 1), 0) & distance) == 0
    for i in range(0, rows, 8):
        tile = value[i : i + 8]
        ahead = pltpu.roll(tile, 8 - distance, 0)
        if distance == 4:
            tiles.append(ahead)
        else:
            tiles.append(jnp.where(lower, ahead, pltpu.roll(tile, distance, 0)))
    return jnp.concatenate(tiles, axis=0)


def swap_into(target, value, step, strides):
    for index, stride in enumerate(strides):

        @pl.when(step == index)
        def _():
            target[...] = swap_rows(value, stride)


def tiled_rows(value, count):
    return jnp.concatenate([value] * count, axis=0)


def forward_kernel(strides, groups, each, core_ref, own_ref, other_ref, order_ref, after_ref,
                   z_ref, kept_ref, trig_ref, now, swapped, dense, angles):
    step = pl.program_id(0)
    width = order_ref.shape[2]
    rows = groups * each
    parts = width // LANES
    stride = lax.shift_right_logical(jnp.int32(strides[0]), step)

    @pl.when(step == 0)
    def _():
        core = core_ref[0]
        tall = each * parts
        for which, ref in ((core, own_ref), (1 - core, other_ref)):
            tokens = ref[:, pl.ds(pl.multiple_of(core * tall, tall), tall), :].astype(F32)
            rest = ref[:, 2 * tall :, :].astype(F32)
            for near in range(groups // 2):
                dense[pl.ds(2 * near + which, 1), :tall] = tokens[near : near + 1]
                dense[pl.ds(2 * near + which, 1), tall:] = rest[near : near + 1]
        for part in range(each + len(strides)):
            for lane in range(parts):
                piece = dense[:, part * parts + lane, :]
                lanes = slice(lane * LANES, (lane + 1) * LANES)
                if part < each:
                    now[part * groups : (part + 1) * groups, lanes] = piece
                else:
                    angles[part - each, :, lanes] = piece

    order, inverse = order_ref[0, 0:1], order_ref[0, 1:2]
    value = jnp.concatenate([now[...], angles[step]], axis=0)
    upper = upper_rows(rows + groups, groups, stride)
    value = jnp.where(upper, permuted(value, order), value)
    swap_into(swapped, value, step, strides)
    turned = value[rows:] + swapped[rows:]
    cosine = jnp.cos(turned)
    sine = jnp.sin(turned)
    sine = jnp.where(upper[rows:], sine, -sine)
    trig_ref[0, :groups] = cosine
    trig_ref[0, groups:] = sine
    value = tiled_rows(cosine, each) * value[:rows] + tiled_rows(sine, each) * swapped[:rows]
    kept_ref[0] = value.astype(BF16)
    value = jnp.where(upper[:rows], permuted(value, inverse), value)
    now[...] = value

    @pl.when(step == len(strides) - 1)
    def _():
        for part in range(each * parts):
            row, lane = part // parts * groups, part % parts * LANES
            dense[:, part, :] = value[row : row + groups, lane : lane + LANES]
        for side in range(z_ref.shape[0]):
            z_ref[side] = dense[:, : each * parts, :].astype(BF16)


def pack_kernel(in_ref, out_ref, dense):
    value = in_ref[...].astype(F32)
    top = jnp.max(jnp.abs(value), axis=(0, 1))
    top = jnp.max(jnp.max(top, axis=0, keepdims=True), axis=1, keepdims=True)
    scale = jnp.ones_like(top)
    exponent = jnp.zeros_like(top)
    for size in STEPS:
        fits = top * scale * 2.0**size < 2.0**15
        scale = jnp.where(fits, scale * 2.0**size, scale)
        exponent = jnp.where(fits, exponent + size, exponent)
    dense[...] = value * scale.reshape(1, 1, 1, 1)
    sides, rows, parts, _ = in_ref.shape
    for part in range(sides * parts):
        out_ref[:, part * LANES : (part + 1) * LANES] = dense[
            part // parts, :, part % parts, :
        ].astype(BF16)
    out_ref[:, sides * parts * LANES :] = jnp.broadcast_to(exponent, (rows, LANES)).astype(BF16)


def pack(array):
    sides, rows, parts, _ = array.shape
    return pl.pallas_call(
        pack_kernel,
        out_shape=jax.ShapeDtypeStruct((rows, (sides * parts + 1) * LANES), BF16),
        scratch_shapes=[pltpu.VMEM(array.shape, F32)],
        name="pack",
    )(array)


def backward_kernel(strides, groups, each, g_ref, kept_ref, trig_ref, order_ref,
                    sum_ref, now, swapped, dense, sums_out):
    step = pl.program_id(0)
    width = kept_ref.shape[2]
    rows = groups * each
    parts = width // LANES
    stride = lax.shift_left(jnp.int32(strides[-1]), step)

    @pl.when(step == 0)
    def _():
        dense[...] = jnp.sum(g_ref[...].astype(F32), axis=0)
        for part in range(each * parts):
            row, lane = part // parts * groups, part % parts * LANES
            now[row : row + groups, lane : lane + LANES] = dense[:, part, :]

    order, inverse = order_ref[0, 0:1], order_ref[0, 1:2]
    upper = upper_rows(rows + groups, groups, stride)
    value = now[...]
    value = jnp.where(upper[:rows], permuted(value, order), value)
    kept = kept_ref[0].astype(F32)
    swap_into(swapped, jnp.concatenate([value, kept], axis=0), step, strides[::-1])
    partner = swapped[:rows]
    terms = partner * kept - value * swapped[rows:]
    sums = terms[:groups]
    for part in range(1, each):
        sums = sums + terms[part * groups : (part + 1) * groups]
    sums = jnp.where(upper[rows:], -sums, sums)
    cosine, sine = trig_ref[0, :groups], trig_ref[0, groups:]
    before = tiled_rows(cosine, each) * value - tiled_rows(sine, each) * partner
    value = jnp.concatenate([before, sums], axis=0)
    value = jnp.where(upper, permuted(value, inverse), value)
    now[...] = value[:rows]
    for index in range(len(strides)):

        @pl.when(step == len(strides) - 1 - index)
        def _():
            for part in range(parts):
                sums_out[:, index * parts + part, :] = value[
                    rows:, part * LANES : (part + 1) * LANES
                ]

    @pl.when(step == len(strides) - 1)
    def _():
        for side in range(sum_ref.shape[0]):
            sum_ref[side] = sums_out[...].astype(BF16)


def turn_forward(strides, groups, each, sides, core, own, other, order, after):
    sections, _, width = order.shape
    rows = groups * each
    near, high, _ = own.shape
    return pl.pallas_call(
        functools.partial(forward_kernel, strides, groups, each),
        grid=(sections,),
        in_specs=[
            pl.BlockSpec(memory_space=pltpu.SMEM),
            pl.BlockSpec((near, high, LANES), lambda s: (0, 0, 0)),
            pl.BlockSpec((near, high, LANES), lambda s: (0, 0, 0)),
            pl.BlockSpec((1, 2, width), lambda s: (s, 0, 0)),
            pl.BlockSpec(memory_space=pl.ANY),
        ],
        out_specs=[
            pl.BlockSpec((sides, groups, each * width // LANES, LANES), lambda s: (0, 0, 0, 0)),
            pl.BlockSpec((1, rows, width), lambda s: (s, 0, 0)),
            pl.BlockSpec((1, 2 * groups, width), lambda s: (s, 0, 0)),
        ],
        out_shape=[
            jax.ShapeDtypeStruct((sides, groups, each * width // LANES, LANES), BF16),
            jax.ShapeDtypeStruct((sections, rows, width), BF16),
            jax.ShapeDtypeStruct((sections, 2 * groups, width), F32),
        ],
        scratch_shapes=[
            pltpu.VMEM((rows, width), F32),
            pltpu.VMEM((rows + groups, width), F32),
            pltpu.VMEM((groups, (each + sections) * width // LANES, LANES), F32),
            pltpu.VMEM((sections, groups, width), F32),
        ],
        compiler_params=pltpu.CompilerParams(vmem_limit_bytes=VMEM),
        cost_estimate=pl.CostEstimate(
            flops=sections * 8 * rows * width * width, bytes_accessed=4 << 20, transcendentals=0
        ),
        name="turn_forward",
    )(core, own, other, order, after)


def turn_backward(strides, groups, each, sides, g, kept, trig, order):
    sections, _, width = order.shape
    rows = groups * each
    last = sections - 1
    return pl.pallas_call(
        functools.partial(backward_kernel, strides, groups, each),
        grid=(sections,),
        in_specs=[
            pl.BlockSpec(g.shape, lambda s: (0, 0, 0, 0)),
            pl.BlockSpec((1, rows, width), lambda s: (last - s, 0, 0)),
            pl.BlockSpec((1, 2 * groups, width), lambda s: (last - s, 0, 0)),
            pl.BlockSpec((1, 2, width), lambda s: (last - s, 0, 0)),
        ],
        out_specs=pl.BlockSpec(
            (sides, groups, sections * width // LANES, LANES), lambda s: (0, 0, 0, 0)
        ),
        out_shape=jax.ShapeDtypeStruct(
            (sides, groups, sections * width // LANES, LANES), BF16
        ),
        scratch_shapes=[
            pltpu.VMEM((rows, width), F32),
            pltpu.VMEM((2 * rows, width), F32),
            pltpu.VMEM(g.shape[1:], F32),
            pltpu.VMEM((groups, sections * width // LANES, LANES), F32),
        ],
        compiler_params=pltpu.CompilerParams(vmem_limit_bytes=VMEM),
        cost_estimate=pl.CostEstimate(
            flops=sections * 8 * rows * width * width, bytes_accessed=4 << 20, transcendentals=0
        ),
        name="turn_backward",
    )(g, kept, trig, order)


def gradient_kernel(core_ref, own_ref, other_ref, weight_ref, after_ref, out_ref):
    near, rows, _ = own_ref.shape
    hidden, width = weight_ref.shape
    core = core_ref[0]
    for which, ref in ((core, own_ref), (1 - core, other_ref)):
        out = product(
            ref[:, :, -hidden:].reshape(near * rows, hidden), weight_ref[...], False
        )
        out_ref[:, pl.ds(which, 1)] = out.astype(BF16).reshape(near, 1, rows, width)


def gradient(core, own, other, weight, after):
    near, rows, lanes = own.shape
    hidden, width = weight.shape
    steps = 2
    return pl.pallas_call(
        gradient_kernel,
        grid=(steps,),
        in_specs=[
            pl.BlockSpec(memory_space=pltpu.SMEM),
            pl.BlockSpec((near, rows // steps, lanes), lambda e: (0, e, 0)),
            pl.BlockSpec((near, rows // steps, lanes), lambda e: (0, e, 0)),
            pl.BlockSpec((hidden, width), lambda e: (0, 0)),
            pl.BlockSpec(memory_space=pl.ANY),
        ],
        out_specs=pl.BlockSpec((near, 2, rows // steps, width), lambda e: (0, 0, e, 0)),
        out_shape=jax.ShapeDtypeStruct((near, 2, rows, width), BF16),
        compiler_params=pltpu.CompilerParams(vmem_limit_bytes=VMEM),
        cost_estimate=pl.CostEstimate(
            flops=4 * near * rows * hidden * width, bytes_accessed=6 << 20, transcendentals=0
        ),
        name="gradient",
    )(core, own, other, weight, after)


def spread_kernel(in_ref, out_ref, dense):
    groups = out_ref.shape[1]
    parts = in_ref.shape[1] // LANES
    own_rows = out_ref.shape[2] // parts
    for side in range(out_ref.shape[0]):
        for row in range(own_rows):
            first = (side * own_rows + row) * groups
            for part in range(parts):
                dense[side, :, row * parts + part, :] = in_ref[
                    first : first + groups, part * LANES : (part + 1) * LANES
                ].astype(F32)
    out_ref[...] = dense[...].astype(BF16)


def spread(array, sides, groups):
    rows, width = array.shape
    shape = (sides, groups, rows // (sides * groups) * width // LANES, LANES)
    return pl.pallas_call(
        spread_kernel,
        out_shape=jax.ShapeDtypeStruct(shape, BF16),
        scratch_shapes=[pltpu.VMEM(shape, F32)],
        name="spread",
    )(array)


def projected_kernel(core_ref, token_ref, exponent_ref, weight_ref, out_ref):
    near, _, few, lanes = token_ref.shape
    width = weight_ref.shape[1]
    parts = lanes // width
    tokens = jnp.concatenate(
        [
            token_ref[:, :, :, part * width : (part + 1) * width].reshape(near * few, width)
            for part in range(parts)
        ],
        axis=0,
    )
    out = product(tokens, weight_ref[...], True)
    exponent = exponent_ref[...].reshape(near * few, LANES)[:, :1].astype(F32)
    scale = jnp.ones_like(exponent)
    for size in STEPS:
        takes = exponent >= size
        scale = jnp.where(takes, scale * 2.0**-size, scale)
        exponent = jnp.where(takes, exponent - size, exponent)
    for part in range(parts):
        piece = (out[part * near * few : (part + 1) * near * few] * scale).astype(BF16)
        piece = piece.reshape(near, few, piece.shape[1])
        out_ref[:, part * few : (part + 1) * few] = piece


def projected_half(core, token_all, weight, each):
    near, _, few, _ = token_all.shape
    hidden, width = weight.shape
    steps = 2
    at_once = each // steps
    in_specs = [
        pl.BlockSpec((near, 1, few, at_once * width), lambda e, c: (0, c[0], 0, e)),
        pl.BlockSpec((near, 1, few, LANES), lambda e, c: (0, c[0], 0, each * width // LANES)),
        pl.BlockSpec((hidden, width), lambda e, c: (0, 0)),
    ]
    operands = [core, token_all, token_all, weight]
    return pl.pallas_call(
        projected_kernel,
        grid_spec=pltpu.PrefetchScalarGridSpec(
            num_scalar_prefetch=1,
            grid=(steps,),
            in_specs=in_specs,
            out_specs=pl.BlockSpec((near, at_once * few, hidden), lambda e, c: (0, e, 0)),
        ),
        out_shape=jax.ShapeDtypeStruct((near, each * few, hidden), BF16),
        compiler_params=pltpu.CompilerParams(vmem_limit_bytes=VMEM),
        cost_estimate=pl.CostEstimate(
            flops=near * few * each * hidden * width // 4, bytes_accessed=1 << 20,
            transcendentals=0,
        ),
        name="projected_half",
    )(*operands)


def sum_kernel(in_ref, out_ref):
    total = jnp.sum(in_ref[...].astype(F32), axis=0).astype(out_ref.dtype)
    for index in range(out_ref.shape[0]):
        out_ref[index] = total


def sum_copies(array, count):
    return pl.pallas_call(
        sum_kernel,
        out_shape=jax.ShapeDtypeStruct((count,) + array.shape[1:], array.dtype),
        name="sum_copies",
    )(array)


def per_device(tokens, up_weight, angles, pair_order, cotangent):
    groups = lax.axis_size(TENSOR)
    near = lax.axis_size(NEAR)
    depth = lax.axis_size(Z)
    sides = lax.axis_size("xh")
    hidden, width = up_weight.shape
    sections = pair_order.shape[0]
    strides = [groups >> (s + 1) for s in range(sections)]
    own_rows = tokens.shape[0] // groups
    each = sides * own_rows
    core = lax.axis_index("c").astype(jnp.int32).reshape(1)
    other_core = [(0, 1), (1, 0)]
    order = with_inverses(pair_order)

    mine = prepare(tokens, angles, cotangent, near)
    cot_own = all_to_all(mine, NEAR)
    cot_other = lax.ppermute(cot_own, "c", other_core)

    part = gradient(core, cot_own, cot_other, up_weight, order)
    summed = lax.psum_scatter(
        part.reshape(depth * part.shape[2], width), Z, scatter_dimension=0, tiled=True
    )

    rotated, kept, trig = turn_forward(
        strides, groups, own_rows, sides, core, cot_own, cot_other, order, part
    )
    back = all_to_all(rotated.reshape((sides * groups,) + rotated.shape[2:]), PLANE)
    back = pack(back.reshape(rotated.shape)).astype(F16)
    token_all = lax.all_gather(back, Z, axis=0, tiled=True).astype(BF16)
    token_all = token_all.reshape(near, 2, groups, each * width + LANES)

    sent = projected_half(1 - core, token_all, up_weight, each)
    arrived = lax.ppermute(sent, "c", other_core)
    both = projected_half(core, token_all, up_weight, each)
    both = (both.astype(F32) + arrived.astype(F32)).astype(BF16)
    projected = lax.psum_scatter(
        both.reshape(near * each * groups, hidden), NEAR, scatter_dimension=0, tiled=True
    )

    g = spread(summed, sides, groups)
    g = all_to_all(g.reshape((sides * groups,) + g.shape[2:]), PLANE).reshape(rotated.shape)
    sums = turn_backward(strides, groups, own_rows, sides, g, kept, trig, order)

    sums = all_to_all(sums.reshape((sides * groups,) + sums.shape[2:]), PLANE)
    sums = all_to_all(sum_copies(sums, depth), Z)
    angle_grads = jnp.sum(sums.astype(F32), axis=0).reshape(sections, width)
    return projected, angle_grads


def solution(mesh):
    fine = jax.sharding.Mesh(
        mesh.devices.reshape(16, 2, 2, 4, 2), ("z", "xh", "xl", "y", "c")
    )
    dp, tensor = ("z", "xh"), TENSOR
    placed = (P(dp, tensor), P(dp, tensor), P(None, tensor), P(), P(tensor, dp))
    return jax.shard_map(
        per_device,
        mesh=fine,
        in_specs=placed,
        out_specs=(P(tensor, dp), P(None, tensor)),
        check_vma=False,
    )
```

```python
import functools

import jax
import jax.numpy as jnp
from jax import lax
from jax.experimental import pallas as pl
from jax.experimental.pallas import tpu as pltpu
from jax.sharding import PartitionSpec as P

BF16 = jnp.bfloat16
F16 = jnp.float16
F32 = jnp.float32
Z = "z"
TENSOR = ("xl", "y", "c")
NEAR = ("xl", "y")
PLANE = ("xh", "xl", "y", "c")
STEPS = (64, 32, 16, 8, 4, 2)
LANES = 128
VMEM = 24 << 20


def all_to_all(array, axes):
    return lax.all_to_all(array, axes, 0, 0, tiled=True)


def product(left, right, transposed):
    dims = (((1,), (1 if transposed else 0,)), ((), ()))
    return lax.dot_general(left, right, dims, preferred_element_type=F32)


def permuted(value, order):
    rows, width = value.shape
    tiles = width // LANES
    out = []
    for to in range(tiles):
        index = order[:, to * LANES : (to + 1) * LANES]
        lane = jnp.broadcast_to(index & (LANES - 1), (rows, LANES))
        tile = jnp.broadcast_to(index // LANES, (rows, LANES))
        chosen = None
        for source in range(tiles):
            piece = jnp.take_along_axis(
                value[:, source * LANES : (source + 1) * LANES],
                lane,
                axis=1,
                mode="promise_in_bounds",
            )
            chosen = piece if chosen is None else jnp.where(tile == source, piece, chosen)
        out.append(chosen)
    return jnp.concatenate(out, axis=1)


def inverse_kernel(column_ref, row_ref, out_ref):
    width, sections = column_ref.shape
    row = lax.broadcasted_iota(jnp.int32, (width, width), 0)
    lane = lax.broadcasted_iota(jnp.int32, (width, width), 1)
    for s in range(sections):
        hits = jnp.where(column_ref[:, s : s + 1] == lane, row, 0)
        out_ref[s, 0:1] = row_ref[s : s + 1]
        out_ref[s, 1:2] = jnp.sum(hits, axis=0, keepdims=True)


def with_inverses(order):
    sections, width = order.shape
    return pl.pallas_call(
        inverse_kernel,
        out_shape=jax.ShapeDtypeStruct((sections, 2, width), jnp.int32),
        compiler_params=pltpu.CompilerParams(vmem_limit_bytes=VMEM),
        name="with_inverses",
    )(order.T, order)


def prepare_kernel(token_ref, angle_ref, cot_ref, out_ref, tokens, dense):
    near = out_ref.shape[0]
    groups, width = 2 * near, token_ref.shape[1]
    own_rows = token_ref.shape[0] // groups
    parts = width // LANES
    for part in range(parts):
        lanes = slice(part * LANES, (part + 1) * LANES)
        tokens[part] = token_ref[:, lanes].astype(F32)
        for core in range(2):
            for row in range(own_rows):
                dense[:, (core * own_rows + row) * parts + part, :] = tokens[
                    part, pl.ds(row * groups + core, near, stride=2), :
                ]
        for s in range(angle_ref.shape[0]):
            dense[:, (2 * own_rows + s) * parts + part, :] = jnp.broadcast_to(
                angle_ref[s : s + 1, lanes], (near, LANES)
            )
    out_ref[:, :, :LANES] = dense[...].astype(BF16)
    for index in range(near):
        out_ref[index, :, LANES:] = cot_ref[...]


def prepare(tokens, angles, cotangent, near):
    rows, hidden = cotangent.shape
    return pl.pallas_call(
        prepare_kernel,
        out_shape=jax.ShapeDtypeStruct((near, rows, LANES + hidden), BF16),
        scratch_shapes=[pltpu.VMEM((tokens.shape[1] // LANES, tokens.shape[0], LANES), F32), pltpu.VMEM((near, rows, LANES), F32)],
        compiler_params=pltpu.CompilerParams(vmem_limit_bytes=60 << 20),
        name="prepare",
    )(tokens, angles, cotangent)


def upper_rows(rows, groups, stride):
    group = lax.broadcasted_iota(jnp.int32, (rows, 1), 0) & (groups - 1)
    return (group & stride) != 0


def swap_rows(value, distance):
    rows = value.shape[0]
    if distance >= 8:
        parts = []
        for i in range(0, rows, 2 * distance):
            parts += [value[i + distance : i + 2 * distance], value[i : i + distance]]
        return jnp.concatenate(parts, axis=0)
    tiles = []
    lower = (lax.broadcasted_iota(jnp.int32, (8, 1), 0) & distance) == 0
    for i in range(0, rows, 8):
        tile = value[i : i + 8]
        ahead = pltpu.roll(tile, 8 - distance, 0)
        if distance == 4:
            tiles.append(ahead)
        else:
            tiles.append(jnp.where(lower, ahead, pltpu.roll(tile, distance, 0)))
    return jnp.concatenate(tiles, axis=0)


def swap_into(target, value, step, strides):
    for index, stride in enumerate(strides):

        @pl.when(step == index)
        def _():
            target[...] = swap_rows(value, stride)


def tiled_rows(value, count):
    return jnp.concatenate([value] * count, axis=0)


def forward_kernel(strides, groups, each, core_ref, own_ref, other_ref, order_ref, after_ref,
                   z_ref, kept_ref, trig_ref, now, swapped, dense, angles):
    step = pl.program_id(0)
    width = order_ref.shape[2]
    rows = groups * each
    parts = width // LANES
    stride = lax.shift_right_logical(jnp.int32(strides[0]), step)

    @pl.when(step == 0)
    def _():
        core = core_ref[0]
        tall = each * parts
        for which, ref in ((core, own_ref), (1 - core, other_ref)):
            tokens = ref[:, pl.ds(pl.multiple_of(core * tall, tall), tall), :].astype(F32)
            rest = ref[:, 2 * tall :, :].astype(F32)
            for near in range(groups // 2):
                dense[pl.ds(2 * near + which, 1), :tall] = tokens[near : near + 1]
                dense[pl.ds(2 * near + which, 1), tall:] = rest[near : near + 1]
        for part in range(each + len(strides)):
            for lane in range(parts):
                piece = dense[:, part * parts + lane, :]
                lanes = slice(lane * LANES, (lane + 1) * LANES)
                if part < each:
                    now[part * groups : (part + 1) * groups, lanes] = piece
                else:
                    angles[part - each, :, lanes] = piece

    order, inverse = order_ref[0, 0:1], order_ref[0, 1:2]
    value = jnp.concatenate([now[...], angles[step]], axis=0)
    upper = upper_rows(rows + groups, groups, stride)
    value = jnp.where(upper, permuted(value, order), value)
    swap_into(swapped, value, step, strides)
    turned = value[rows:] + swapped[rows:]
    cosine = jnp.cos(turned)
    sine = jnp.sin(turned)
    sine = jnp.where(upper[rows:], sine, -sine)
    trig_ref[0, :groups] = cosine
    trig_ref[0, groups:] = sine
    value = tiled_rows(cosine, each) * value[:rows] + tiled_rows(sine, each) * swapped[:rows]
    kept_ref[0] = value.astype(BF16)
    value = jnp.where(upper[:rows], permuted(value, inverse), value)
    now[...] = value

    @pl.when(step == len(strides) - 1)
    def _():
        for part in range(each * parts):
            row, lane = part // parts * groups, part % parts * LANES
            dense[:, part, :] = value[row : row + groups, lane : lane + LANES]
        for side in range(z_ref.shape[0]):
            z_ref[side] = dense[:, : each * parts, :].astype(BF16)


def pack_kernel(in_ref, out_ref, dense):
    value = in_ref[...].astype(F32)
    top = jnp.max(jnp.abs(value), axis=(0, 1))
    top = jnp.max(jnp.max(top, axis=0, keepdims=True), axis=1, keepdims=True)
    scale = jnp.ones_like(top)
    exponent = jnp.zeros_like(top)
    for size in STEPS:
        fits = top * scale * 2.0**size < 2.0**15
        scale = jnp.where(fits, scale * 2.0**size, scale)
        exponent = jnp.where(fits, exponent + size, exponent)
    dense[...] = value * scale.reshape(1, 1, 1, 1)
    sides, rows, parts, _ = in_ref.shape
    for part in range(sides * parts):
        out_ref[:, part * LANES : (part + 1) * LANES] = dense[
            part // parts, :, part % parts, :
        ].astype(BF16)
    out_ref[:, sides * parts * LANES :] = jnp.broadcast_to(exponent, (rows, LANES)).astype(BF16)


def pack(array):
    sides, rows, parts, _ = array.shape
    return pl.pallas_call(
        pack_kernel,
        out_shape=jax.ShapeDtypeStruct((rows, (sides * parts + 1) * LANES), BF16),
        scratch_shapes=[pltpu.VMEM(array.shape, F32)],
        name="pack",
    )(array)


def backward_kernel(strides, groups, each, g_ref, kept_ref, trig_ref, order_ref,
                    sum_ref, now, swapped, dense, sums_out):
    step = pl.program_id(0)
    width = kept_ref.shape[2]
    rows = groups * each
    parts = width // LANES
    stride = lax.shift_left(jnp.int32(strides[-1]), step)

    @pl.when(step == 0)
    def _():
        dense[...] = jnp.sum(g_ref[...].astype(F32), axis=0)
        for part in range(each * parts):
            row, lane = part // parts * groups, part % parts * LANES
            now[row : row + groups, lane : lane + LANES] = dense[:, part, :]

    order, inverse = order_ref[0, 0:1], order_ref[0, 1:2]
    upper = upper_rows(rows + groups, groups, stride)
    value = now[...]
    value = jnp.where(upper[:rows], permuted(value, order), value)
    kept = kept_ref[0].astype(F32)
    swap_into(swapped, jnp.concatenate([value, kept], axis=0), step, strides[::-1])
    partner = swapped[:rows]
    terms = partner * kept - value * swapped[rows:]
    sums = terms[:groups]
    for part in range(1, each):
        sums = sums + terms[part * groups : (part + 1) * groups]
    sums = jnp.where(upper[rows:], -sums, sums)
    cosine, sine = trig_ref[0, :groups], trig_ref[0, groups:]
    before = tiled_rows(cosine, each) * value - tiled_rows(sine, each) * partner
    value = jnp.concatenate([before, sums], axis=0)
    value = jnp.where(upper, permuted(value, inverse), value)
    now[...] = value[:rows]
    for index in range(len(strides)):

        @pl.when(step == len(strides) - 1 - index)
        def _():
            for part in range(parts):
                sums_out[:, index * parts + part, :] = value[
                    rows:, part * LANES : (part + 1) * LANES
                ]

    @pl.when(step == len(strides) - 1)
    def _():
        for side in range(sum_ref.shape[0]):
            sum_ref[side] = sums_out[...].astype(BF16)


def turn_forward(strides, groups, each, sides, core, own, other, order, after):
    sections, _, width = order.shape
    rows = groups * each
    near, high, _ = own.shape
    return pl.pallas_call(
        functools.partial(forward_kernel, strides, groups, each),
        grid=(sections,),
        in_specs=[
            pl.BlockSpec(memory_space=pltpu.SMEM),
            pl.BlockSpec((near, high, LANES), lambda s: (0, 0, 0)),
            pl.BlockSpec((near, high, LANES), lambda s: (0, 0, 0)),
            pl.BlockSpec((1, 2, width), lambda s: (s, 0, 0)),
            pl.BlockSpec(memory_space=pl.ANY),
        ],
        out_specs=[
            pl.BlockSpec((sides, groups, each * width // LANES, LANES), lambda s: (0, 0, 0, 0)),
            pl.BlockSpec((1, rows, width), lambda s: (s, 0, 0)),
            pl.BlockSpec((1, 2 * groups, width), lambda s: (s, 0, 0)),
        ],
        out_shape=[
            jax.ShapeDtypeStruct((sides, groups, each * width // LANES, LANES), BF16),
            jax.ShapeDtypeStruct((sections, rows, width), BF16),
            jax.ShapeDtypeStruct((sections, 2 * groups, width), F32),
        ],
        scratch_shapes=[
            pltpu.VMEM((rows, width), F32),
            pltpu.VMEM((rows + groups, width), F32),
            pltpu.VMEM((groups, (each + sections) * width // LANES, LANES), F32),
            pltpu.VMEM((sections, groups, width), F32),
        ],
        compiler_params=pltpu.CompilerParams(vmem_limit_bytes=VMEM),
        cost_estimate=pl.CostEstimate(
            flops=sections * 8 * rows * width * width, bytes_accessed=4 << 20, transcendentals=0
        ),
        name="turn_forward",
    )(core, own, other, order, after)


def turn_backward(strides, groups, each, sides, g, kept, trig, order):
    sections, _, width = order.shape
    rows = groups * each
    last = sections - 1
    return pl.pallas_call(
        functools.partial(backward_kernel, strides, groups, each),
        grid=(sections,),
        in_specs=[
            pl.BlockSpec(g.shape, lambda s: (0, 0, 0, 0)),
            pl.BlockSpec((1, rows, width), lambda s: (last - s, 0, 0)),
            pl.BlockSpec((1, 2 * groups, width), lambda s: (last - s, 0, 0)),
            pl.BlockSpec((1, 2, width), lambda s: (last - s, 0, 0)),
        ],
        out_specs=pl.BlockSpec(
            (sides, groups, sections * width // LANES, LANES), lambda s: (0, 0, 0, 0)
        ),
        out_shape=jax.ShapeDtypeStruct(
            (sides, groups, sections * width // LANES, LANES), BF16
        ),
        scratch_shapes=[
            pltpu.VMEM((rows, width), F32),
            pltpu.VMEM((2 * rows, width), F32),
            pltpu.VMEM(g.shape[1:], F32),
            pltpu.VMEM((groups, sections * width // LANES, LANES), F32),
        ],
        compiler_params=pltpu.CompilerParams(vmem_limit_bytes=VMEM),
        cost_estimate=pl.CostEstimate(
            flops=sections * 8 * rows * width * width, bytes_accessed=4 << 20, transcendentals=0
        ),
        name="turn_backward",
    )(g, kept, trig, order)


def gradient_kernel(core_ref, own_ref, other_ref, weight_ref, after_ref, out_ref):
    near, rows, _ = own_ref.shape
    hidden, width = weight_ref.shape
    core = core_ref[0]
    for which, ref in ((core, own_ref), (1 - core, other_ref)):
        out = product(
            ref[:, :, -hidden:].reshape(near * rows, hidden), weight_ref[...], False
        )
        out_ref[:, pl.ds(which, 1)] = out.astype(BF16).reshape(near, 1, rows, width)


def gradient(core, own, other, weight, after):
    near, rows, lanes = own.shape
    hidden, width = weight.shape
    steps = 2
    return pl.pallas_call(
        gradient_kernel,
        grid=(steps,),
        in_specs=[
            pl.BlockSpec(memory_space=pltpu.SMEM),
            pl.BlockSpec((near, rows // steps, lanes), lambda e: (0, e, 0)),
            pl.BlockSpec((near, rows // steps, lanes), lambda e: (0, e, 0)),
            pl.BlockSpec((hidden, width), lambda e: (0, 0)),
            pl.BlockSpec(memory_space=pl.ANY),
        ],
        out_specs=pl.BlockSpec((near, 2, rows // steps, width), lambda e: (0, 0, e, 0)),
        out_shape=jax.ShapeDtypeStruct((near, 2, rows, width), BF16),
        compiler_params=pltpu.CompilerParams(vmem_limit_bytes=VMEM),
        cost_estimate=pl.CostEstimate(
            flops=4 * near * rows * hidden * width, bytes_accessed=6 << 20, transcendentals=0
        ),
        name="gradient",
    )(core, own, other, weight, after)


def spread_kernel(in_ref, out_ref, dense):
    groups = out_ref.shape[1]
    parts = in_ref.shape[1] // LANES
    own_rows = out_ref.shape[2] // parts
    for side in range(out_ref.shape[0]):
        for row in range(own_rows):
            first = (side * own_rows + row) * groups
            for part in range(parts):
                dense[side, :, row * parts + part, :] = in_ref[
                    first : first + groups, part * LANES : (part + 1) * LANES
                ].astype(F32)
    out_ref[...] = dense[...].astype(BF16)


def spread(array, sides, groups):
    rows, width = array.shape
    shape = (sides, groups, rows // (sides * groups) * width // LANES, LANES)
    return pl.pallas_call(
        spread_kernel,
        out_shape=jax.ShapeDtypeStruct(shape, BF16),
        scratch_shapes=[pltpu.VMEM(shape, F32)],
        name="spread",
    )(array)


def projected_kernel(core_ref, token_ref, exponent_ref, weight_ref, out_ref):
    near, _, few, lanes = token_ref.shape
    width = weight_ref.shape[1]
    parts = lanes // width
    tokens = jnp.concatenate(
        [
            token_ref[:, :, :, part * width : (part + 1) * width].reshape(near * few, width)
            for part in range(parts)
        ],
        axis=0,
    )
    out = product(tokens, weight_ref[...], True)
    exponent = exponent_ref[...].reshape(near * few, LANES)[:, :1].astype(F32)
    scale = jnp.ones_like(exponent)
    for size in STEPS:
        takes = exponent >= size
        scale = jnp.where(takes, scale * 2.0**-size, scale)
        exponent = jnp.where(takes, exponent - size, exponent)
    for part in range(parts):
        piece = (out[part * near * few : (part + 1) * near * few] * scale).astype(BF16)
        piece = piece.reshape(near, few, piece.shape[1])
        out_ref[:, part * few : (part + 1) * few] = piece


def projected_half(core, token_all, weight, each):
    near, _, few, _ = token_all.shape
    hidden, width = weight.shape
    steps = 1
    at_once = each // steps
    in_specs = [
        pl.BlockSpec((near, 1, few, at_once * width), lambda e, c: (0, c[0], 0, e)),
        pl.BlockSpec((near, 1, few, LANES), lambda e, c: (0, c[0], 0, each * width // LANES)),
        pl.BlockSpec((hidden, width), lambda e, c: (0, 0)),
    ]
    operands = [core, token_all, token_all, weight]
    return pl.pallas_call(
        projected_kernel,
        grid_spec=pltpu.PrefetchScalarGridSpec(
            num_scalar_prefetch=1,
            grid=(steps,),
            in_specs=in_specs,
            out_specs=pl.BlockSpec((near, at_once * few, hidden), lambda e, c: (0, e, 0)),
        ),
        out_shape=jax.ShapeDtypeStruct((near, each * few, hidden), BF16),
        compiler_params=pltpu.CompilerParams(vmem_limit_bytes=VMEM),
        cost_estimate=pl.CostEstimate(
            flops=near * few * each * hidden * width // 4, bytes_accessed=1 << 20,
            transcendentals=0,
        ),
        name="projected_half",
    )(*operands)


def sum_kernel(in_ref, out_ref):
    total = jnp.sum(in_ref[...].astype(F32), axis=0).astype(out_ref.dtype)
    for index in range(out_ref.shape[0]):
        out_ref[index] = total


def sum_copies(array, count):
    return pl.pallas_call(
        sum_kernel,
        out_shape=jax.ShapeDtypeStruct((count,) + array.shape[1:], array.dtype),
        name="sum_copies",
    )(array)


def per_device(tokens, up_weight, angles, pair_order, cotangent):
    groups = lax.axis_size(TENSOR)
    near = lax.axis_size(NEAR)
    depth = lax.axis_size(Z)
    sides = lax.axis_size("xh")
    hidden, width = up_weight.shape
    sections = pair_order.shape[0]
    strides = [groups >> (s + 1) for s in range(sections)]
    own_rows = tokens.shape[0] // groups
    each = sides * own_rows
    core = lax.axis_index("c").astype(jnp.int32).reshape(1)
    other_core = [(0, 1), (1, 0)]
    order = with_inverses(pair_order)

    mine = prepare(tokens, angles, cotangent, near)
    cot_own = all_to_all(mine, NEAR)
    cot_other = lax.ppermute(cot_own, "c", other_core)

    part = gradient(core, cot_own, cot_other, up_weight, order)
    summed = lax.psum_scatter(
        part.reshape(depth * part.shape[2], width), Z, scatter_dimension=0, tiled=True
    )

    rotated, kept, trig = turn_forward(
        strides, groups, own_rows, sides, core, cot_own, cot_other, order, part
    )
    back = all_to_all(rotated.reshape((sides * groups,) + rotated.shape[2:]), PLANE)
    back = pack(back.reshape(rotated.shape)).astype(F16)
    token_all = lax.all_gather(back, Z, axis=0, tiled=True).astype(BF16)
    token_all = token_all.reshape(near, 2, groups, each * width + LANES)

    sent = projected_half(1 - core, token_all, up_weight, each)
    arrived = lax.ppermute(sent, "c", other_core)
    both = projected_half(core, token_all, up_weight, each)
    both = (both.astype(F32) + arrived.astype(F32)).astype(BF16)
    projected = lax.psum_scatter(
        both.reshape(near * each * groups, hidden), NEAR, scatter_dimension=0, tiled=True
    )

    g = spread(summed, sides, groups)
    g = all_to_all(g.reshape((sides * groups,) + g.shape[2:]), PLANE).reshape(rotated.shape)
    sums = turn_backward(strides, groups, own_rows, sides, g, kept, trig, order)

    sums = all_to_all(sums.reshape((sides * groups,) + sums.shape[2:]), PLANE)
    sums = all_to_all(sum_copies(sums, depth), Z)
    angle_grads = jnp.sum(sums.astype(F32), axis=0).reshape(sections, width)
    return projected, angle_grads


def solution(mesh):
    fine = jax.sharding.Mesh(
        mesh.devices.reshape(16, 2, 2, 4, 2), ("z", "xh", "xl", "y", "c")
    )
    dp, tensor = ("z", "xh"), TENSOR
    placed = (P(dp, tensor), P(dp, tensor), P(None, tensor), P(), P(tensor, dp))
    return jax.shard_map(
        per_device,
        mesh=fine,
        in_specs=placed,
        out_specs=(P(tensor, dp), P(None, tensor)),
        check_vma=False,
    )
```
